256 devices in a mesh: seq: 16 (over z, core), chan: 16 (over y, x).
Axes of the slice: x: 4, y: 4, z: 8, core: 2. Of those that a mesh axis runs over, the one named last changes fastest.
Arguments:
- tokens: bfloat16 [4096, 4096], P('seq', 'chan'), may hold values from -6 to 6
- in_weight: bfloat16 [4096, 3, 4096], P(None, None, 'chan'), may hold values from -0.09375 to 0.09375
- short_taps: float32 [3, 3, 4096], P(None, None, 'chan'), may hold values from -3.5 to 3.5
- filter_in: float32 [33, 64], replicated, may hold values from -1.5 to 1.5
- filter_out: float32 [64, 4096], P(None, 'chan'), may hold values from -0.75 to 0.75
- rates: float32 [4096], P('chan'), may hold values from 1.2207031e-05 to 0.034
- skip: float32 [4096], P('chan'), may hold values from -1 to 1
- out_weight: bfloat16 [4096, 4096], P('chan'), may hold values from -0.09375 to 0.09375
Outputs:
- mixed: bfloat16 [4096, 4096], P('seq', 'chan')
The draws below stay inside these ranges and needn't reach their ends.
All inputs are finite; a program needn't handle non-finite values.
Results may differ from the reference program's by a relative error of at most 0.02.
Values may be sent and summed in bfloat16 or wider, within the bound.
A program may use at most 128 MiB of HBM per device.

```python
import math
import jax
import jax.numpy as jnp
from jax import lax

D = 4096
ORDER = 64
TAPS = 3
EMB = 33
TOTAL = 4096


def draw_filter_in(key, part):
    key = jax.random.fold_in(key, 11)
    sign_key, size_key = jax.random.split(key)
    sign_part = jnp.where(jax.random.bernoulli(sign_key, 0.5, (EMB, ORDER)), 1.0, -1.0).astype(jnp.float32)
    magnitude = jax.random.uniform(size_key, (EMB, ORDER), jnp.float32, 0.5, 1.5)
    return sign_part * magnitude


def draw_rates(key, part):
    key = jax.random.fold_in(key, 23)
    pick_key, fast_key, slow_key = jax.random.split(key, 3)
    fast_rates = jnp.exp(jax.random.uniform(fast_key, (D,), jnp.float32, math.log(0.02), math.log(1.0 / 30.0)))
    slow_low = 0.05 / TOTAL
    slow_high = 2.0 / TOTAL
    fast_share = 0.125
    slow_rates = jnp.exp(jax.random.uniform(slow_key, (D,), jnp.float32, math.log(slow_low), math.log(slow_high)))
    picked = jax.random.uniform(pick_key, (D,), jnp.float32) < fast_share
    return jnp.where(picked, fast_rates, slow_rates).astype(jnp.float32)


def levels(stream_key, dims, pieces, low, top_value):
    loudness, own = 1.0, jax.random.fold_in(stream_key, 6)
    for dim, blocks in pieces:
        draws = jnp.exp(jax.random.uniform(jax.random.fold_in(own, dim), (blocks,), jnp.float32, low / len(pieces), top_value / len(pieces)))
        loudness = loudness * jnp.repeat(draws, dims[dim] // blocks).reshape([-1 if axis == dim else 1 for axis in range(len(dims))])
    return loudness


def bell_draw(rng, dims, deviation, limit, cuts=(), kind=jnp.bfloat16):
    entries = jax.random.normal(rng, dims, jnp.float32) * deviation
    if len(cuts) > 0:
        entries = levels(rng, dims, cuts, -0.22, 0.18) * entries
    return jnp.clip(entries, min=-limit, max=limit).astype(kind)


def setup_inputs(seed: int = 0) -> dict:
    key_list = jax.random.split(jax.random.key(seed), 9)
    return {
        "tokens": bell_draw(key_list[0], (TOTAL, D), 1.0, 6.0, ((0, 16), (1, 16))),
        "in_weight": bell_draw(key_list[1], (D, 3, D), D ** -0.5, 0.09375, ((2, 16),)),
        "short_taps": bell_draw(key_list[2], (TAPS, 3, D), TAPS ** -0.5, 3.5, ((2, 16),), jnp.float32),
        "filter_in": draw_filter_in(jax.random.fold_in(key_list[8], 71), 0),
        "filter_out": bell_draw(key_list[4], (ORDER, D), ORDER ** -0.5, 0.75, ((1, 16),), jnp.float32),
        "rates": draw_rates(jax.random.fold_in(key_list[8], 71), 0),
        "skip": jnp.clip(jax.random.uniform(key_list[6], (D,), jnp.float32, -1.0, 1.0) * levels(key_list[6], (D,), ((0, 16),), -0.4, 0.0), -1.0, 1.0),
        "out_weight": bell_draw(key_list[7], (D, D), D ** -0.5, 0.09375, ((0, 16),)),
    }


def filter_values(positions, seq_total, filter_in, filter_out, rates):
    freq_count = (filter_in.shape[0] - 1) // 2
    freqs = 1 + jnp.arange(freq_count, dtype=jnp.int32) * (seq_total // 4 - 1) // (freq_count - 1)
    phase = positions[:, None] * freqs[None, :] % seq_total
    angle = phase.astype(jnp.float32) * (2.0 * math.pi / seq_total)
    places = positions.astype(jnp.float32)
    feats = jnp.concatenate([places[:, None] / seq_total, jnp.cos(angle), jnp.sin(angle)], axis=1)
    inner = jnp.sin(jnp.dot(feats, filter_in, precision=lax.Precision.HIGHEST))
    shaped = jnp.dot(inner, filter_out, precision=lax.Precision.HIGHEST)
    return shaped * jnp.sqrt(rates)[None, :] * jnp.exp(-rates[None, :] * places[:, None])

def reference(tokens, in_weight, short_taps, filter_in, filter_out, rates, skip, out_weight):
    seq_total = tokens.shape[0]
    model_width = tokens.shape[1]
    flat_weight = in_weight.reshape(model_width, 3 * model_width)
    projected = jnp.dot(tokens, flat_weight, preferred_element_type=jnp.float32).astype(jnp.bfloat16)
    projected = projected.reshape(seq_total, 3, model_width)
    padded = jnp.concatenate([jnp.zeros((2, 3, model_width), jnp.bfloat16), projected], axis=0).astype(jnp.float32)
    branch = jnp.zeros((seq_total, 3, model_width), jnp.float32)
    for lag in range(3):
        branch = branch + short_taps[lag][None] * padded[2 - lag:2 - lag + seq_total]
    query = branch[:, 0]
    drive = (branch[:, 1] * branch[:, 2]).astype(jnp.bfloat16)
    drive_f = drive.astype(jnp.float32)
    filt = filter_values(jnp.arange(seq_total, dtype=jnp.int32), seq_total, filter_in, filter_out, rates)
    length = 2 * seq_total
    spectrum = jnp.fft.rfft(drive_f, n=length, axis=0) * jnp.fft.rfft(filt, n=length, axis=0)
    conv = jnp.fft.irfft(spectrum, n=length, axis=0)[:seq_total]
    conv = conv + skip[None, :] * drive_f
    gated = (query * conv).astype(jnp.bfloat16)
    return jnp.dot(gated, out_weight, preferred_element_type=jnp.float32).astype(jnp.bfloat16)
```

```python
import functools
import math

import jax
import jax.numpy as jnp
import ml_dtypes
import numpy as np
from jax import lax
from jax.experimental import pallas as pl
from jax.experimental.pallas import tpu as pltpu
from jax.sharding import PartitionSpec as P

BLOCK = 256
GROUP = 16
BLOCKS = 16
FREQS = 2 * BLOCK
FEAT_ROWS = 40
MESH_ID = pl.DeviceIdType.MESH
F32 = jnp.float32
BF16 = jnp.bfloat16


def split_two(values):
    high = values.astype(ml_dtypes.bfloat16)
    low = (values - high.astype(np.float64)).astype(ml_dtypes.bfloat16)
    return np.stack([high, low])


@functools.cache
def tables(total):
    row = np.arange(BLOCK)
    freq = np.arange(BLOCK)
    angle = 2.0 * np.pi * ((row[:, None] * freq[None, :]) % FREQS) / FREQS
    imag = -np.sin(angle)
    imag[:, 0] = 1.0 - 2.0 * (row % 2)
    forward = np.concatenate([np.cos(angle), imag], axis=1)
    angle = 2.0 * np.pi * ((freq[:, None] * (row[None, :] + BLOCK)) % FREQS) / FREQS
    real_rows = 2.0 * np.cos(angle)
    real_rows[0] = 1.0
    imag_rows = -2.0 * np.sin(angle)
    imag_rows[0] = 1.0 - 2.0 * (row % 2)
    inverse = np.concatenate([real_rows, imag_rows], axis=0) / FREQS
    place = np.arange(total)
    count = 16
    rates = 1 + np.arange(count) * (total // 4 - 1) // (count - 1)
    phase = (place[None, :] * rates[:, None]) % total
    turn = 2.0 * np.pi * phase / total
    feats = np.zeros((FEAT_ROWS, total), np.float32)
    feats[0] = place / total
    feats[1 : 1 + count] = np.cos(turn)
    feats[1 + count : 1 + 2 * count] = np.sin(turn)
    return split_two(forward), split_two(inverse), feats


def sine(x):
    turns = jnp.round(x * (1.0 / math.pi))
    r = x - turns * 3.140625
    r = r - turns * 0.0009670257568359375
    r = r - turns * 6.2771141529083252e-07
    odd = turns - 2.0 * jnp.floor(turns * 0.5)
    z = r * r
    poly = 1.0 / 6227020800.0
    for term in (-39916800.0, 362880.0, -5040.0, 120.0, -6.0):
        poly = poly * z + 1.0 / term
    value = r + r * z * poly
    return value * (1.0 - 2.0 * odd)


def dot(a, b):
    return jnp.dot(a, b, preferred_element_type=F32)


def halves(x):
    high = x.astype(BF16)
    return high, (x - high.astype(F32)).astype(BF16)


def slot(h, first, second):
    dx, dy = (first, second) if h == 0 else (second, first)
    return (dy % 4) * 4 + dx % 4


def rows(h, part):
    base = h * 128
    return {"f": (base, 128), "q1": (base, 64), "q2": (base + 64, 64)}[part]


class Links:
    def __init__(self, send, recv):
        self.send, self.recv, self.known = send, recv, {}

    def start(self, name, src, dst, device):
        index = len(self.known)
        copy = pltpu.make_async_remote_copy(
            src_ref=src,
            dst_ref=dst,
            send_sem=self.send.at[index],
            recv_sem=self.recv.at[index],
            device_id=device,
            device_id_type=MESH_ID,
        )
        copy.start()
        self.known[name] = copy

    def arrived(self, name):
        self.known[name].wait_recv()

    def finish(self):
        for copy in self.known.values():
            copy.wait_send()


def kernel(
    tok, win, taps, fin, fout, rates, skip, wout, feats, fmat, gmat,
    out,
    xbuf, wbuf, wo, featbuf, fbuf, gbuf, acc, finp, fot, ratecol, skipcol, fs, aspec, sre, sim, sre2,
    pbuf, pf, qbuf, drv, sbuf, dbuf, xs, ys, cbuf, rbuf, gated,
    part, snd, rq, rh, psnd, rpq, rph, red,
    local_sem, w_sem, wo_sem, ag_send, ag_recv, halo_send, halo_recv, a_send, a_recv, b_send, b_recv, rs_send, rs_recv,
):
    s = lax.axis_index("seq")
    c = lax.axis_index("chan")
    x, y = lax.rem(c, 4), lax.div(c, 4)
    spots = [(dx, dy) for dy in range(4) for dx in range(4)]

    def chan_at(dx, dy):
        return lax.rem(y + dy + 4, 4) * 4 + lax.rem(x + dx + 4, 4)

    def neighbour(h, stage, sign):
        along_x = (h == 0) == (stage == 0)
        return {"chan": chan_at(sign, 0) if along_x else chan_at(0, sign)}

    own = pltpu.make_async_copy(tok, xbuf.at[0], local_sem.at[0])
    own.start()
    order = [(0, 0), (1, 0), (3, 0), (0, 1), (0, 3), (2, 0), (0, 2), (1, 1), (1, 3), (3, 1), (3, 3),
             (1, 2), (3, 2), (2, 1), (2, 3), (2, 2)]
    w_copies = {}
    feat_copy = pltpu.make_async_copy(feats, featbuf, local_sem.at[1])
    f_copy = pltpu.make_async_copy(fmat, fbuf, local_sem.at[2])
    g_copy = pltpu.make_async_copy(gmat, gbuf, local_sem.at[3])
    feat_copy.start()
    for n, (dx, dy) in enumerate(order):
        at = pl.ds(pl.multiple_of(chan_at(-dx, -dy) * BLOCK, BLOCK), BLOCK)
        w_copies[dx, dy] = pltpu.make_async_copy(win.at[:, at, :], wbuf.at[n], w_sem.at[n])
        w_copies[dx, dy].start()
        if n == 1:
            f_copy.start()
    g_copy.start()
    wo_copies = {}
    for n, (dx, dy) in enumerate(spots):
        at = pl.ds(pl.multiple_of(chan_at(dx, dy) * BLOCK, BLOCK), BLOCK)
        wo_copies[dx, dy] = pltpu.make_async_copy(wout.at[:, at], wo.at[n], wo_sem.at[n])
        wo_copies[dx, dy].start()

    barrier = pltpu.get_barrier_semaphore()
    for device in (chan_at(1, 0), chan_at(-1, 0), chan_at(0, 1), chan_at(0, -1)):
        pl.semaphore_signal(barrier, inc=1, device_id={"chan": device}, device_id_type=MESH_ID)
    for k in range(1, BLOCKS):
        pl.semaphore_signal(
            barrier, inc=1, device_id={"seq": lax.rem(s + k, BLOCKS)}, device_id_type=MESH_ID
        )
    pl.semaphore_wait(barrier, 4 + BLOCKS - 1)

    links = Links(ag_send, ag_recv)

    def push(name, h, frm, to, piece, stage, sign, src=None):
        start, size = rows(h, piece)
        here = (xbuf.at[slot(h, *frm)] if src is None else src).at[pl.ds(start, size), :]
        there = xbuf.at[slot(h, *to), pl.ds(start, size), :]
        links.start((name, h), here, there, neighbour(h, stage, sign))

    def take(*names):
        for name in names:
            for h in (0, 1):
                links.arrived((name, h))

    def multiply(blocks, first=False):
        for dx, dy in blocks:
            w_copies[dx, dy].wait()
        for j in range(3):
            total = None if first else acc[j]
            for dx, dy in blocks:
                term = dot(xbuf[dy * 4 + dx], wbuf[order.index((dx, dy)), j])
                total = term if total is None else total + term
            acc[j] = total

    for h in (0, 1):
        push("P0+", h, (0, 0), (1, 0), "f", 0, 1, tok)
        push("P0-", h, (0, 0), (3, 0), "f", 0, -1, tok)
    for h in (0, 1):
        push("Q00+", h, (0, 0), (0, 1), "f", 1, 1, tok)
        push("Q00-", h, (0, 0), (0, 3), "f", 1, -1, tok)

    finp[...] = jnp.zeros_like(finp)
    finp[0:33, 0:64] = fin[...]
    fin_t = jnp.transpose(finp[...])[0:64, 0:FEAT_ROWS]
    fot[...] = jnp.transpose(fout[...])
    ratecol[...] = jnp.transpose(jnp.broadcast_to(rates[...], (128, BLOCK)))
    skipcol[...] = jnp.transpose(jnp.broadcast_to(skip[...], (128, BLOCK)))
    mine = pl.ds(pl.multiple_of(s * GROUP, GROUP), GROUP)
    fo = fot[mine, :]
    rate = ratecol[mine, :]
    rate = jnp.concatenate([rate] * 4, axis=1)
    scale = jnp.sqrt(rate)
    feat_copy.wait()

    def filter_piece(n, carry):
        at = pl.ds(pl.multiple_of(n * 512, 512), 512)
        arg = jnp.dot(fin_t, featbuf[:, at], precision=lax.Precision.HIGHEST, preferred_element_type=F32)
        shaped = jnp.dot(fo, sine(arg), precision=lax.Precision.HIGHEST, preferred_element_type=F32)
        place = (lax.broadcasted_iota(jnp.int32, (GROUP, 512), 1) + n * 512).astype(F32)
        value = shaped * scale * jnp.exp(-rate * place)
        fs[pl.ds(pl.multiple_of(n * 32, 32), GROUP), :] = value[:, :BLOCK]
        fs[pl.ds(pl.multiple_of(n * 32 + 16, 16), GROUP), :] = value[:, BLOCK:]
        return carry

    lax.fori_loop(0, 8, filter_piece, 0)
    own.wait()
    multiply([(0, 0)], first=True)

    take("P0+", "P0-")
    for h in (0, 1):
        push("P1+", h, (1, 0), (2, 0), "q1", 0, 1)
        push("P1-", h, (3, 0), (2, 0), "q2", 0, -1)
    for h in (0, 1):
        for dp in (1, 3):
            push(f"Q{dp}0+", h, (dp, 0), (dp, 1), "f", 1, 1)
            push(f"Q{dp}0-", h, (dp, 0), (dp, 3), "f", 1, -1)
    take("Q00+", "Q00-")
    for h in (0, 1):
        push("Q01+", h, (0, 1), (0, 2), "q1", 1, 1)
        push("Q01-", h, (0, 3), (0, 2), "q2", 1, -1)
    multiply([(1, 0), (3, 0), (0, 1), (0, 3)])

    take("P1+", "P1-")
    for h in (0, 1):
        push("Q2a+", h, (2, 0), (2, 1), "q1", 1, 1)
        push("Q2a-", h, (2, 0), (2, 3), "q1", 1, -1)
        push("Q2b+", h, (2, 0), (2, 1), "q2", 1, 1)
        push("Q2b-", h, (2, 0), (2, 3), "q2", 1, -1)

    f_copy.wait()
    high, low = halves(fs[...])
    aspec[0:GROUP, :] = jnp.zeros((GROUP, FREQS), F32)
    aspec[GROUP:, :] = dot(high, fbuf[0]) + dot(low, fbuf[0]) + dot(high, fbuf[1])
    lane = lax.broadcasted_iota(jnp.int32, (GROUP, BLOCK), 1)
    parity = 1.0 - 2.0 * lax.rem(lane, 2).astype(F32)

    def lag_piece(n, carry):
        before = pl.ds(pl.multiple_of(n * GROUP, GROUP), GROUP)
        after = pl.ds(pl.multiple_of(n * GROUP + GROUP, GROUP), GROUP)
        re = aspec[before, 0:BLOCK] + parity * aspec[after, 0:BLOCK]
        im = aspec[before, BLOCK:] + parity * aspec[after, BLOCK:]
        sre[before, :] = re
        sim[before, :] = jnp.where(lane == 0, 0.0, im)
        sre2[before, :] = jnp.where(lane == 0, im, re)
        return carry

    lax.fori_loop(0, BLOCKS, lag_piece, 0)

    for dp in (1, 3):
        take(f"Q{dp}0+", f"Q{dp}0-")
        for h in (0, 1):
            push(f"Q{dp}1+", h, (dp, 1), (dp, 2), "q1", 1, 1)
            push(f"Q{dp}1-", h, (dp, 3), (dp, 2), "q2", 1, -1)
    take("Q01+", "Q01-")
    multiply([(2, 0), (0, 2)])
    take("Q2a+", "Q2b-")
    for h in (0, 1):
        push("Q21+", h, (2, 1), (2, 2), "q1", 1, 1)
        push("Q21-", h, (2, 3), (2, 2), "q2", 1, -1)
    multiply([(1, 1), (1, 3), (3, 1), (3, 3)])
    take("Q2a-", "Q2b+", "Q11+", "Q11-", "Q31+", "Q31-")
    multiply([(1, 2), (3, 2), (2, 1), (2, 3)])
    take("Q21+", "Q21-")
    multiply([(2, 2)])

    for j in range(3):
        rounded = acc[j].astype(BF16)
        pbuf[j, 16:, :] = rounded
        pf[j, 16:, :] = rounded.astype(F32)
    halo = pltpu.make_async_remote_copy(
        src_ref=pbuf.at[:, pl.ds(BLOCK, 16), :],
        dst_ref=pbuf.at[:, pl.ds(0, 16), :],
        send_sem=halo_send.at[0],
        recv_sem=halo_recv.at[0],
        device_id={"seq": lax.rem(s + 1, BLOCKS)},
        device_id_type=MESH_ID,
    )
    halo.start()

    def short(start, size):
        branch = []
        for j in range(3):
            value = taps[0, pl.ds(j, 1), :] * pf[j, pl.ds(16 + start, size), :]
            value = value + taps[1, pl.ds(j, 1), :] * pf[j, pl.ds(15 + start, size), :]
            branch.append(value + taps[2, pl.ds(j, 1), :] * pf[j, pl.ds(14 + start, size), :])
        qbuf[pl.ds(start, size), :] = branch[0]
        drv[pl.ds(start, size), :] = branch[1] * branch[2]

    for start in range(16, BLOCK, 16):
        short(start, 16)
    halo.wait_recv()
    live = (s > 0).astype(F32)
    for j in range(3):
        pf[j, 0:16, :] = pbuf[j, 0:16, :].astype(F32) * live
    short(0, 16)

    sbuf[...] = jnp.transpose(drv[...]).astype(BF16).reshape(BLOCKS, GROUP, BLOCK)

    def exchange(src, dst, send, recv):
        copies = []
        for k in range(1, BLOCKS):
            other = lax.rem(s + k, BLOCKS)
            copy = pltpu.make_async_remote_copy(
                src_ref=src.at[other],
                dst_ref=dst.at[s],
                send_sem=send.at[k],
                recv_sem=recv.at[k],
                device_id={"seq": other},
                device_id_type=MESH_ID,
            )
            copy.start()
            copies.append(copy)
        dst[pl.ds(s, 1)] = src[pl.ds(s, 1)]
        for copy in copies:
            copy.wait_recv()
        return copies

    waits = [halo] + exchange(sbuf, dbuf, a_send, a_recv)

    drive = dbuf[...].reshape(BLOCK, BLOCK)
    xs[...] = dot(drive, fbuf[0]) + dot(drive, fbuf[1])

    def spectrum(i, carry):
        def lag(d, total):
            at = pl.ds(pl.multiple_of((i - d) * GROUP, GROUP), GROUP)
            by = pl.ds(pl.multiple_of(d * GROUP, GROUP), GROUP)
            xr, xi = xs[at, 0:BLOCK], xs[at, BLOCK:]
            im = sim[by, :]
            return (
                total[0] + xr * sre[by, :] - xi * im,
                total[1] + xr * im + xi * sre2[by, :],
            )

        zero = jnp.zeros((GROUP, BLOCK), F32)
        re, im = lax.fori_loop(0, i + 1, lag, (zero, zero))
        to = pl.ds(pl.multiple_of(i * GROUP, GROUP), GROUP)
        ys[to, 0:BLOCK] = re
        ys[to, BLOCK:] = im
        return carry

    lax.fori_loop(0, BLOCKS, spectrum, 0)
    g_copy.wait()
    high, low = halves(ys[...])
    conv = dot(high, gbuf[0]) + dot(low, gbuf[0]) + dot(high, gbuf[1])
    direct = skipcol[mine, :]
    direct = jnp.concatenate([direct, direct], axis=1)
    conv = conv.reshape(BLOCKS, GROUP, BLOCK) + direct[None] * dbuf[...].astype(F32)
    cbuf[...] = conv.astype(BF16)
    waits += exchange(cbuf, rbuf, b_send, b_recv)

    back = jnp.transpose(rbuf[...].reshape(BLOCK, BLOCK).astype(F32))
    gated[...] = (qbuf[...] * back).astype(BF16)

    sums = Links(rs_send, rs_recv)

    def project(dx, dy):
        wo_copies[dx, dy].wait()
        part[dy * 4 + dx] = dot(gated[...], wo[dy * 4 + dx])

    def far(h, dp):
        start, _ = rows(h, "f")
        snd[h, dp, 0] = part[slot(h, dp, 2), pl.ds(start, 128), :].astype(BF16)
        sums.start(("Q1+", h, dp), snd.at[h, dp, 0, pl.ds(0, 64), :], rq.at[h, dp, 0], neighbour(h, 1, 1))
        sums.start(("Q1-", h, dp), snd.at[h, dp, 0, pl.ds(64, 64), :], rq.at[h, dp, 1], neighbour(h, 1, -1))

    project(2, 2)
    far(0, 2)
    far(1, 2)
    for n in (1, 3):
        project(n, 2)
        far(0, n)
        project(2, n)
        far(1, n)
    project(0, 2)
    far(0, 0)
    project(2, 0)
    far(1, 0)
    for dx, dy in ((1, 1), (1, 3), (3, 1), (3, 3), (0, 1), (1, 0), (0, 3), (3, 0), (0, 0)):
        project(dx, dy)

    for dp in (2, 1, 3, 0):
        for h in (0, 1):
            base = h * 128
            sums.arrived(("Q1+", h, dp))
            one = part.at[slot(h, dp, 1)]
            snd[h, dp, 1, 0:64] = (one[pl.ds(base, 64), :] + rq[h, dp, 0].astype(F32)).astype(BF16)
            snd[h, dp, 1, 64:128] = one[pl.ds(base + 64, 64), :].astype(BF16)
            sums.start(("Q2+", h, dp), snd.at[h, dp, 1], rh.at[h, dp, 0], neighbour(h, 1, 1))
            sums.arrived(("Q1-", h, dp))
            one = part.at[slot(h, dp, 3)]
            snd[h, dp, 2, 0:64] = one[pl.ds(base, 64), :].astype(BF16)
            snd[h, dp, 2, 64:128] = (one[pl.ds(base + 64, 64), :] + rq[h, dp, 1].astype(F32)).astype(BF16)
            sums.start(("Q2-", h, dp), snd.at[h, dp, 2], rh.at[h, dp, 1], neighbour(h, 1, -1))

    def reduced(h, dp):
        sums.arrived(("Q2+", h, dp))
        sums.arrived(("Q2-", h, dp))
        return (
            part[slot(h, dp, 0), pl.ds(h * 128, 128), :]
            + rh[h, dp, 0].astype(F32)
            + rh[h, dp, 1].astype(F32)
        )

    for h in (0, 1):
        psnd[h, 0] = reduced(h, 2).astype(BF16)
        sums.start(("P1+", h), psnd.at[h, 0, pl.ds(0, 64), :], rpq.at[h, 0], neighbour(h, 0, 1))
        sums.start(("P1-", h), psnd.at[h, 0, pl.ds(64, 64), :], rpq.at[h, 1], neighbour(h, 0, -1))
    for dp, n in ((1, 0), (3, 1), (0, 2)):
        for h in (0, 1):
            red[h, n] = reduced(h, dp)
    for h in (0, 1):
        sums.arrived(("P1+", h))
        psnd[h, 1, 0:64] = (red[h, 0, 0:64] + rpq[h, 0].astype(F32)).astype(BF16)
        psnd[h, 1, 64:128] = red[h, 0, 64:128].astype(BF16)
        sums.start(("P2+", h), psnd.at[h, 1], rph.at[h, 0], neighbour(h, 0, 1))
        sums.arrived(("P1-", h))
        psnd[h, 2, 0:64] = red[h, 1, 0:64].astype(BF16)
        psnd[h, 2, 64:128] = (red[h, 1, 64:128] + rpq[h, 1].astype(F32)).astype(BF16)
        sums.start(("P2-", h), psnd.at[h, 2], rph.at[h, 1], neighbour(h, 0, -1))
    for h in (0, 1):
        sums.arrived(("P2+", h))
        sums.arrived(("P2-", h))
        total = red[h, 2] + rph[h, 0].astype(F32) + rph[h, 1].astype(F32)
        out[h * 128 : h * 128 + 128, :] = total.astype(BF16)

    links.finish()
    sums.finish()
    for copy in waits:
        copy.wait_send()


def per_device(tokens, in_weight, short_taps, filter_in, filter_out, rates, skip, out_weight):
    forward, inverse, feats = tables(4096)
    vmem = pl.BlockSpec(memory_space=pltpu.VMEM)
    hbm = pl.BlockSpec(memory_space=pl.ANY)
    dma = pltpu.SemaphoreType.DMA
    square = (BLOCK, BLOCK)
    scratch = [
        pltpu.VMEM((16, *square), BF16),
        pltpu.VMEM((16, 3, *square), BF16),
        pltpu.VMEM((16, *square), BF16),
        pltpu.VMEM((FEAT_ROWS, 4096), F32),
        pltpu.VMEM((2, BLOCK, FREQS), BF16),
        pltpu.VMEM((2, FREQS, BLOCK), BF16),
        pltpu.VMEM((3, *square), F32),
        pltpu.VMEM((128, 128), F32),
        pltpu.VMEM((BLOCK, 64), F32),
        pltpu.VMEM((BLOCK, 128), F32),
        pltpu.VMEM((BLOCK, 128), F32),
        pltpu.VMEM(square, F32),
        pltpu.VMEM((GROUP + BLOCK, FREQS), F32),
        pltpu.VMEM(square, F32),
        pltpu.VMEM(square, F32),
        pltpu.VMEM(square, F32),
        pltpu.VMEM((3, 16 + BLOCK, BLOCK), BF16),
        pltpu.VMEM((3, 16 + BLOCK, BLOCK), F32),
        pltpu.VMEM(square, F32),
        pltpu.VMEM(square, F32),
        pltpu.VMEM((BLOCKS, GROUP, BLOCK), BF16),
        pltpu.VMEM((BLOCKS, GROUP, BLOCK), BF16),
        pltpu.VMEM((BLOCK, FREQS), F32),
        pltpu.VMEM((BLOCK, FREQS), F32),
        pltpu.VMEM((BLOCKS, GROUP, BLOCK), BF16),
        pltpu.VMEM((BLOCKS, GROUP, BLOCK), BF16),
        pltpu.VMEM(square, BF16),
        pltpu.VMEM((16, *square), F32),
        pltpu.VMEM((2, 4, 3, 128, BLOCK), BF16),
        pltpu.VMEM((2, 4, 2, 64, BLOCK), BF16),
        pltpu.VMEM((2, 4, 2, 128, BLOCK), BF16),
        pltpu.VMEM((2, 3, 128, BLOCK), BF16),
        pltpu.VMEM((2, 2, 64, BLOCK), BF16),
        pltpu.VMEM((2, 2, 128, BLOCK), BF16),
        pltpu.VMEM((2, 3, 128, BLOCK), F32),
        dma((4,)),
        dma((16,)),
        dma((16,)),
        dma((44,)),
        dma((44,)),
        dma((1,)),
        dma((1,)),
        dma((16,)),
        dma((16,)),
        dma((16,)),
        dma((16,)),
        dma((40,)),
        dma((40,)),
    ]
    return pl.pallas_call(
        kernel,
        out_shape=jax.ShapeDtypeStruct(square, BF16),
        in_specs=[hbm, hbm, vmem, vmem, vmem, vmem, vmem, hbm, hbm, hbm, hbm],
        out_specs=vmem,
        scratch_shapes=scratch,
        compiler_params=pltpu.CompilerParams(
            collective_id=0, has_side_effects=True, vmem_limit_bytes=56 * 1024 * 1024
        ),
        name="hyena",
    )(
        tokens,
        jnp.transpose(in_weight, (1, 0, 2)),
        short_taps,
        filter_in,
        filter_out,
        rates.reshape(1, BLOCK),
        skip.reshape(1, BLOCK),
        out_weight,
        jnp.asarray(feats),
        jnp.asarray(forward),
        jnp.asarray(inverse),
    )


def solution(mesh):
    placed = (
        P("seq", "chan"),
        P(None, None, "chan"),
        P(None, None, "chan"),
        P(),
        P(None, "chan"),
        P("chan"),
        P("chan"),
        P("chan", None),
    )
    return jax.shard_map(
        per_device, mesh=mesh, in_specs=placed, out_specs=P("seq", "chan"), check_vma=False
    )
```

```python
import functools
import math

import jax
import jax.numpy as jnp
import ml_dtypes
import numpy as np
from jax import lax
from jax.experimental import pallas as pl
from jax.experimental.pallas import tpu as pltpu
from jax.sharding import PartitionSpec as P

BLOCK = 256
GROUP = 16
BLOCKS = 16
FREQS = 2 * BLOCK
FEAT_ROWS = 40
EDGE = 16
LAG_STEP = 4
LAG_PAD = (LAG_STEP - 1) * GROUP
ORDER = (8, 7, 9, 6, 10, 5, 11, 4, 12, 3, 13, 2, 14, 1, 15)
MESH_ID = pl.DeviceIdType.MESH
F32 = jnp.float32
BF16 = jnp.bfloat16


def split_two(values):
    high = values.astype(ml_dtypes.bfloat16)
    low = (values - high.astype(np.float64)).astype(ml_dtypes.bfloat16)
    return np.stack([high, low])


@functools.cache
def tables(total):
    row = np.arange(BLOCK)
    freq = np.arange(BLOCK)
    angle = 2.0 * np.pi * ((row[:, None] * freq[None, :]) % FREQS) / FREQS
    imag = -np.sin(angle)
    imag[:, 0] = 1.0 - 2.0 * (row % 2)
    forward = np.concatenate([np.cos(angle), imag], axis=1)
    angle = 2.0 * np.pi * ((freq[:, None] * (row[None, :] + BLOCK)) % FREQS) / FREQS
    real_rows = 2.0 * np.cos(angle)
    real_rows[0] = 1.0
    imag_rows = -2.0 * np.sin(angle)
    imag_rows[0] = 1.0 - 2.0 * (row % 2)
    inverse = np.concatenate([real_rows, imag_rows], axis=0) / FREQS
    place = np.arange(total)
    count = 16
    rates = 1 + np.arange(count) * (total // 4 - 1) // (count - 1)
    phase = (place[None, :] * rates[:, None]) % total
    turn = 2.0 * np.pi * phase / total
    feats = np.zeros((FEAT_ROWS, total), np.float32)
    feats[0] = place / total
    feats[1 : 1 + count] = np.cos(turn)
    feats[1 + count : 1 + 2 * count] = np.sin(turn)
    return split_two(forward), split_two(inverse), feats


def sine(x):
    turns = jnp.round(x * (1.0 / math.pi))
    r = x - turns * 3.140625
    r = r - turns * 0.0009670257568359375
    r = r - turns * 6.2771141529083252e-07
    odd = turns - 2.0 * jnp.floor(turns * 0.5)
    z = r * r
    poly = 1.0 / 6227020800.0
    for term in (-39916800.0, 362880.0, -5040.0, 120.0, -6.0):
        poly = poly * z + 1.0 / term
    value = r + r * z * poly
    return value * (1.0 - 2.0 * odd)


def dot(a, b):
    return jnp.dot(a, b, preferred_element_type=F32)


def halves(x):
    high = x.astype(BF16)
    return high, (x - high.astype(F32)).astype(BF16)


def slot(h, first, second):
    dx, dy = (first, second) if h == 0 else (second, first)
    return (dy % 4) * 4 + dx % 4


def rows(h, part):
    base = h * 128
    cut = EDGE if h else 0
    return {"f": (base, 128 - cut), "q1": (base, 64), "q2": (base + 64, 64 - cut)}[part]


class Links:
    def __init__(self, send, recv):
        self.send, self.recv, self.known = send, recv, {}

    def start(self, name, src, dst, device):
        index = len(self.known)
        copy = pltpu.make_async_remote_copy(
            src_ref=src,
            dst_ref=dst,
            send_sem=self.send.at[index],
            recv_sem=self.recv.at[index],
            device_id=device,
            device_id_type=MESH_ID,
        )
        copy.start()
        self.known[name] = copy

    def arrived(self, name):
        self.known[name].wait_recv()

    def finish(self):
        for copy in self.known.values():
            copy.wait_send()


def kernel(
    tok, win, taps_in, fin_in, fout_in, rates_in, skip_in, wout, feats, fmat, gmat,
    out,
    taps, fin, fout, rates, skip, xbuf, wbuf, wo, featbuf, fbuf, gbuf, acc, finp, fot, ratecol, skipcol, fs, aspec, sre, sim, sre2,
    edge_out, edge_in, pf, qbuf, drv, sbuf, dbuf, xs, ys, cbuf, rbuf, gated,
    part, far_snd, far_rcv, snd, rq, rh, psnd, rp, red,
    word_sem, local_sem, w_sem, wo_sem, ag_send, ag_recv, halo_send, halo_recv, a_send, a_recv, b_send, b_recv, rs_send, rs_recv,
):
    s = lax.axis_index("seq")
    c = lax.axis_index("chan")
    x, y = lax.rem(c, 4), lax.div(c, 4)
    spots = [(dx, dy) for dy in range(4) for dx in range(4)]

    def chan_at(dx, dy):
        return lax.rem(y + dy + 4, 4) * 4 + lax.rem(x + dx + 4, 4)

    def neighbour(h, stage, sign):
        along_x = (h == 0) == (stage == 0)
        return {"chan": chan_at(sign, 0) if along_x else chan_at(0, sign)}

    small = [
        pltpu.make_async_copy(src, dst, local_sem.at[4 + n])
        for n, (src, dst) in enumerate(
            ((fin_in, fin), (fout_in, fout), (rates_in, rates), (skip_in, skip), (taps_in, taps))
        )
    ]
    for copy in small:
        copy.start()
    own = pltpu.make_async_copy(tok, xbuf.at[0], local_sem.at[0])
    own.start()
    order = [(0, 0), (1, 0), (3, 0), (0, 1), (0, 3), (2, 0), (0, 2), (1, 1), (1, 3), (3, 1), (3, 3),
             (1, 2), (2, 1), (3, 2), (2, 3), (2, 2)]
    w_copies = {}
    feat_copy = pltpu.make_async_copy(feats, featbuf, local_sem.at[1])
    f_copy = pltpu.make_async_copy(fmat, fbuf, local_sem.at[2])
    g_copy = pltpu.make_async_copy(gmat, gbuf, local_sem.at[3])
    feat_copy.start()
    for n, (dx, dy) in enumerate(order):
        at = pl.ds(pl.multiple_of(chan_at(-dx, -dy) * BLOCK, BLOCK), BLOCK)
        w_copies[dx, dy] = pltpu.make_async_copy(win.at[:, at, :], wbuf.at[n], w_sem.at[n])
        w_copies[dx, dy].start()
        if n == 1:
            f_copy.start()
    g_copy.start()
    wo_copies = {}
    for n, (dx, dy) in enumerate(spots):
        at = pl.ds(pl.multiple_of(chan_at(dx, dy) * BLOCK, BLOCK), BLOCK)
        wo_copies[dx, dy] = pltpu.make_async_copy(wout.at[:, at], wo.at[n], wo_sem.at[n])
        wo_copies[dx, dy].start()

    z, core = lax.div(s, 2), lax.rem(s, 2)

    def plane(step):
        return {"seq": lax.rem(z + step + 8, 8) * 2 + core}

    sibling = {"seq": z * 2 + 1 - core}
    barrier = pltpu.get_barrier_semaphore()
    near = [{"chan": chan_at(step, 0)} for step in (1, -1, 2)]
    near += [{"chan": chan_at(0, step)} for step in (1, -1, 2)]
    near += [sibling, plane(1), plane(-1)]
    for device in near:
        pl.semaphore_signal(barrier, inc=1, device_id=device, device_id_type=MESH_ID)
    pl.semaphore_wait(barrier, len(near))

    rounds = ([plane(1), plane(-1)], [plane(2), plane(-2)], [sibling])

    def tell(n):
        for device in rounds[n]:
            pl.semaphore_signal(word_sem.at[n], inc=1, device_id=device, device_id_type=MESH_ID)

    def hear(n):
        pl.semaphore_wait(word_sem.at[n], len(rounds[n]))

    links = Links(ag_send, ag_recv)

    def push(name, h, frm, to, piece, stage, sign, src=None):
        start, size = rows(h, piece)
        here = (xbuf.at[slot(h, *frm)] if src is None else src).at[pl.ds(start, size), :]
        there = xbuf.at[slot(h, *to), pl.ds(start, size), :]
        links.start((name, h), here, there, neighbour(h, stage, sign))

    def take(*names):
        for name in names:
            for h in (0, 1):
                links.arrived((name, h))

    def multiply(blocks, first=False):
        for dx, dy in blocks:
            if order.index((dx, dy)) < 3:
                w_copies[dx, dy].wait()
        for j in range(3):
            total = None if first else acc[j]
            for dx, dy in blocks:
                term = dot(xbuf[dy * 4 + dx], wbuf[order.index((dx, dy)), j])
                total = term if total is None else total + term
            acc[j] = total

    tell(0)
    for h in (0, 1):
        push("P2", h, (0, 0), (2, 0), "f", 0, 2, tok)
        push("P0+", h, (0, 0), (1, 0), "f", 0, 1, tok)
        push("P0-", h, (0, 0), (3, 0), "f", 0, -1, tok)
    edge = pl.ds(BLOCK - EDGE, EDGE)
    for step in (1, 2, 3):
        links.start(("EP", step), tok.at[edge, :], xbuf.at[step, edge, :], {"chan": chan_at(step, 0)})
    for h in (0, 1):
        push("Q00+", h, (0, 0), (0, 1), "f", 1, 1, tok)
        push("Q00-", h, (0, 0), (0, 3), "f", 1, -1, tok)

    for copy in small:
        copy.wait()
    finp[...] = jnp.zeros_like(finp)
    finp[0:33, 0:64] = fin[...]
    fin_t = jnp.transpose(finp[...])[0:64, 0:FEAT_ROWS]
    fot[...] = jnp.transpose(fout[...])
    ratecol[...] = jnp.transpose(jnp.broadcast_to(rates[...], (128, BLOCK)))
    skipcol[...] = jnp.transpose(jnp.broadcast_to(skip[...], (128, BLOCK)))
    mine = pl.ds(pl.multiple_of(s * GROUP, GROUP), GROUP)
    fo = fot[mine, :]
    rate = ratecol[mine, :]
    rate = jnp.concatenate([rate] * 4, axis=1)
    scale = jnp.sqrt(rate)
    feat_copy.wait()

    def filter_piece(n, carry):
        at = pl.ds(pl.multiple_of(n * 512, 512), 512)
        arg = jnp.dot(fin_t, featbuf[:, at], precision=lax.Precision.HIGHEST, preferred_element_type=F32)
        shaped = jnp.dot(fo, sine(arg), precision=lax.Precision.HIGHEST, preferred_element_type=F32)
        place = (lax.broadcasted_iota(jnp.int32, (GROUP, 512), 1) + n * 512).astype(F32)
        value = shaped * scale * jnp.exp(-rate * place)
        fs[pl.ds(pl.multiple_of(n * 32, 32), GROUP), :] = value[:, :BLOCK]
        fs[pl.ds(pl.multiple_of(n * 32 + 16, 16), GROUP), :] = value[:, BLOCK:]
        return carry

    lax.fori_loop(0, 8, filter_piece, 0)
    own.wait()
    multiply([(0, 0)], first=True)

    take("P0+", "P0-")
    for h in (0, 1):
        for dp in (1, 3):
            push(f"Q{dp}0+", h, (dp, 0), (dp, 1), "f", 1, 1)
            push(f"Q{dp}0-", h, (dp, 0), (dp, 3), "f", 1, -1)
    for step in (1, 2, 3):
        links.arrived(("EP", step))
    row = xbuf.at[pl.ds(0, 4), edge, :]
    for step in (1, 2, 3):
        links.start(("EQ", step), row, xbuf.at[pl.ds(4 * step, 4), edge, :], {"chan": chan_at(0, step)})
    take("P2")
    for h in (0, 1):
        push("Q20+", h, (2, 0), (2, 1), "f", 1, 1)
        push("Q20-", h, (2, 0), (2, 3), "f", 1, -1)
    take("Q00+", "Q00-")
    for h in (0, 1):
        push("Q01+", h, (0, 1), (0, 2), "q1", 1, 1)
        push("Q01-", h, (0, 3), (0, 2), "q2", 1, -1)
    hear(0)
    tell(1)
    multiply([(1, 0), (3, 0)])
    for dp in (1, 3):
        take(f"Q{dp}0+", f"Q{dp}0-")
        for h in (0, 1):
            push(f"Q{dp}1+", h, (dp, 1), (dp, 2), "q1", 1, 1)
            push(f"Q{dp}1-", h, (dp, 3), (dp, 2), "q2", 1, -1)

    for step in (1, 2, 3):
        links.arrived(("EQ", step))
    for dx, dy in order[3:]:
        w_copies[dx, dy].wait()
    for j in range(3):
        total = None
        for dx, dy in order:
            term = dot(xbuf[dy * 4 + dx, BLOCK - EDGE :, :], wbuf[order.index((dx, dy)), j])
            total = term if total is None else total + term
        edge_out[j] = total.astype(BF16)
    halo = pltpu.make_async_remote_copy(
        src_ref=edge_out,
        dst_ref=edge_in,
        send_sem=halo_send.at[0],
        recv_sem=halo_recv.at[0],
        device_id={"seq": lax.rem(s + 1, BLOCKS)},
        device_id_type=MESH_ID,
    )
    halo.start()
    hear(1)
    tell(2)
    take("Q20+", "Q20-")
    for h in (0, 1):
        push("Q21+", h, (2, 1), (2, 2), "q1", 1, 1)
        push("Q21-", h, (2, 3), (2, 2), "q2", 1, -1)

    f_copy.wait()
    high, low = halves(fs[...])
    aspec[0:GROUP, :] = jnp.zeros((GROUP, FREQS), F32)
    aspec[GROUP:, :] = dot(high, fbuf[0]) + dot(low, fbuf[0]) + dot(high, fbuf[1])
    lane = lax.broadcasted_iota(jnp.int32, (GROUP, BLOCK), 1)
    parity = 1.0 - 2.0 * lax.rem(lane, 2).astype(F32)

    for table in (sre, sim, sre2):
        table[BLOCK:, :] = jnp.zeros((LAG_PAD, BLOCK), F32)

    def lag_piece(n, carry):
        before = pl.ds(pl.multiple_of(n * GROUP, GROUP), GROUP)
        after = pl.ds(pl.multiple_of(n * GROUP + GROUP, GROUP), GROUP)
        re = aspec[before, 0:BLOCK] + parity * aspec[after, 0:BLOCK]
        im = aspec[before, BLOCK:] + parity * aspec[after, BLOCK:]
        sre[before, :] = re
        sim[before, :] = jnp.where(lane == 0, 0.0, im)
        sre2[before, :] = jnp.where(lane == 0, im, re)
        return carry

    lax.fori_loop(0, BLOCKS, lag_piece, 0)

    take("Q01+", "Q01-")
    multiply([(0, 1), (0, 3), (2, 0), (0, 2), (1, 1), (1, 3), (3, 1), (3, 3)])
    for h, dp, block in ((0, 1, (1, 2)), (1, 1, (2, 1)), (0, 3, (3, 2)), (1, 3, (2, 3))):
        links.arrived((f"Q{dp}1+", h))
        links.arrived((f"Q{dp}1-", h))
        multiply([block])
    hear(2)
    take("Q21+", "Q21-")
    multiply([(2, 2)])

    for j in range(3):
        pf[j, 16:, :] = acc[j].astype(BF16).astype(F32)

    def short(start, size):
        branch = []
        for j in range(3):
            value = taps[0, pl.ds(j, 1), :] * pf[j, pl.ds(16 + start, size), :]
            value = value + taps[1, pl.ds(j, 1), :] * pf[j, pl.ds(15 + start, size), :]
            branch.append(value + taps[2, pl.ds(j, 1), :] * pf[j, pl.ds(14 + start, size), :])
        qbuf[pl.ds(start, size), :] = branch[0]
        drv[pl.ds(start, size), :] = branch[1] * branch[2]

    halo.wait_recv()
    live = (s > 0).astype(F32)
    for j in range(3):
        pf[j, 0:16, :] = edge_in[j].astype(F32) * live
    for start in range(0, BLOCK, 32):
        short(start, 32)

    sbuf[...] = jnp.transpose(drv[...]).astype(BF16).reshape(BLOCKS, GROUP, BLOCK)

    def give(k, src, dst, send, recv):
        other = lax.rem(s + k, BLOCKS)
        copy = pltpu.make_async_remote_copy(
            src_ref=src,
            dst_ref=dst.at[s],
            send_sem=send.at[k],
            recv_sem=recv.at[k],
            device_id={"seq": other},
            device_id_type=MESH_ID,
        )
        copy.start()
        return copy

    gone = [give(k, sbuf.at[lax.rem(s + k, BLOCKS)], dbuf, a_send, a_recv) for k in ORDER]
    dbuf[pl.ds(s, 1)] = sbuf[pl.ds(s, 1)]
    xs[0:LAG_PAD, :] = jnp.zeros((LAG_PAD, FREQS), F32)
    direct = skipcol[mine, :]
    direct = jnp.concatenate([direct, direct], axis=1)
    g_copy.wait()
    for copy in gone:
        copy.wait_recv()
    waits = [halo] + gone

    drive = dbuf[...].reshape(BLOCK, BLOCK)
    xs[LAG_PAD:, :] = dot(drive, fbuf[0]) + dot(drive, fbuf[1])

    def spectrum(n, i):
        def lags(turn, total):
            re, im = total
            for d in range(LAG_STEP):
                d = turn * LAG_STEP + d
                at = pl.ds(pl.multiple_of((i - d) * GROUP + LAG_PAD, GROUP), GROUP)
                by = pl.ds(pl.multiple_of(d * GROUP, GROUP), GROUP)
                xr, xi = xs[at, 0:BLOCK], xs[at, BLOCK:]
                part_im = sim[by, :]
                re = re + (xr * sre[by, :] - xi * part_im)
                im = im + (xr * part_im + xi * sre2[by, :])
            return re, im

        zero = jnp.zeros((GROUP, BLOCK), F32)
        re, im = lax.fori_loop(0, lax.div(i + LAG_STEP, LAG_STEP), lags, (zero, zero))
        ys[n * GROUP : (n + 1) * GROUP, 0:BLOCK] = re
        ys[n * GROUP : (n + 1) * GROUP, BLOCK:] = im

    steps = ORDER + (0,)
    for start in (0, 8):
        for n in range(start, start + 8):
            spectrum(n, lax.rem(s + steps[n], BLOCKS))
        some = slice(start * GROUP, start * GROUP + 8 * GROUP)
        high, low = halves(ys[some, :])
        both = dot(jnp.concatenate([high, low], axis=0), gbuf[0])
        conv = both[: 8 * GROUP] + both[8 * GROUP :] + dot(high, gbuf[1])
        for n in range(start, start + 8):
            i = lax.rem(s + steps[n], BLOCKS)
            value = conv[(n - start) * GROUP : (n - start + 1) * GROUP, :]
            cbuf[n] = (value + direct * dbuf[i].astype(F32)).astype(BF16)
            if steps[n]:
                waits.append(give(steps[n], cbuf.at[n], rbuf, b_send, b_recv))
    rbuf[pl.ds(s, 1)] = cbuf[pl.ds(BLOCKS - 1, 1)]
    for copy in waits[-15:]:
        copy.wait_recv()

    back = jnp.transpose(rbuf[...].reshape(BLOCK, BLOCK).astype(F32))
    gated[...] = (qbuf[...] * back).astype(BF16)

    sums = Links(rs_send, rs_recv)

    def project(dx, dy):
        wo_copies[dx, dy].wait()
        part[dy * 4 + dx] = dot(gated[...], wo[dy * 4 + dx])

    def half(h, dp, dq):
        return part.at[slot(h, dp, dq), pl.ds(h * 128, 128), :]

    def straight(h, n):
        dq, sign = ((2, 2), (1, 1), (3, -1))[n]
        far_snd[h, n] = half(h, 2, dq)[...].astype(BF16)
        sums.start(("F", h, n), far_snd.at[h, n], far_rcv.at[h, n], neighbour(h, 1, sign))

    def relay(h, e):
        snd[h, e, 0] = half(h, (1, 3, 0)[e], 2)[...].astype(BF16)
        sums.start(("Q1+", h, e), snd.at[h, e, 0, pl.ds(0, 64), :], rq.at[h, e, 0], neighbour(h, 1, 1))
        sums.start(("Q1-", h, e), snd.at[h, e, 0, pl.ds(64, 64), :], rq.at[h, e, 1], neighbour(h, 1, -1))

    for n in (1, 3):
        project(n, 2)
        relay(0, (n - 1) // 2)
        project(2, n)
        relay(1, (n - 1) // 2)
    project(2, 2)
    for h in (0, 1):
        for n in (0, 1, 2):
            straight(h, n)
    project(0, 2)
    relay(0, 2)
    project(2, 0)
    relay(1, 2)
    for dx, dy in ((1, 1), (1, 3), (3, 1), (3, 3), (0, 1), (1, 0), (0, 3), (3, 0), (0, 0)):
        project(dx, dy)

    for e in (0, 1, 2):
        dp = (1, 3, 0)[e]
        for h in (0, 1):
            sums.arrived(("Q1+", h, e))
            one = half(h, dp, 1)
            snd[h, e, 1, 0:64] = (one[0:64, :] + rq[h, e, 0].astype(F32)).astype(BF16)
            snd[h, e, 1, 64:128] = one[64:128, :].astype(BF16)
            sums.start(("Q2+", h, e), snd.at[h, e, 1], rh.at[h, e, 0], neighbour(h, 1, 1))
            sums.arrived(("Q1-", h, e))
            one = half(h, dp, 3)
            snd[h, e, 2, 0:64] = one[0:64, :].astype(BF16)
            snd[h, e, 2, 64:128] = (one[64:128, :] + rq[h, e, 1].astype(F32)).astype(BF16)
            sums.start(("Q2-", h, e), snd.at[h, e, 2], rh.at[h, e, 1], neighbour(h, 1, -1))
    for h in (0, 1):
        total = half(h, 2, 0)[...]
        for n in (1, 2, 0):
            sums.arrived(("F", h, n))
            total = total + far_rcv[h, n].astype(F32)
        psnd[h, 0] = total.astype(BF16)
        sums.start(("P", h, 0), psnd.at[h, 0], rp.at[h, 0], neighbour(h, 0, 2))

    def reduced(h, e):
        sums.arrived(("Q2+", h, e))
        sums.arrived(("Q2-", h, e))
        return half(h, (1, 3, 0)[e], 0)[...] + rh[h, e, 0].astype(F32) + rh[h, e, 1].astype(F32)

    for e, sign in ((0, 1), (1, -1)):
        for h in (0, 1):
            psnd[h, 1 + e] = reduced(h, e).astype(BF16)
            sums.start(("P", h, 1 + e), psnd.at[h, 1 + e], rp.at[h, 1 + e], neighbour(h, 0, sign))
    for h in (0, 1):
        red[h] = reduced(h, 2)
    for h in (0, 1):
        total = red[h]
        for n in (0, 1, 2):
            sums.arrived(("P", h, n))
            total = total + rp[h, n].astype(F32)
        out[h * 128 : h * 128 + 128, :] = total.astype(BF16)

    links.finish()
    sums.finish()
    for copy in waits:
        copy.wait_send()


def per_device(tokens, in_weight, short_taps, filter_in, filter_out, rates, skip, out_weight):
    forward, inverse, feats = tables(4096)
    vmem = pl.BlockSpec(memory_space=pltpu.VMEM)
    hbm = pl.BlockSpec(memory_space=pl.ANY)
    dma = pltpu.SemaphoreType.DMA
    square = (BLOCK, BLOCK)
    scratch = [
        pltpu.VMEM((3, 3, BLOCK), F32),
        pltpu.VMEM((33, 64), F32),
        pltpu.VMEM((64, BLOCK), F32),
        pltpu.VMEM((1, BLOCK), F32),
        pltpu.VMEM((1, BLOCK), F32),
        pltpu.VMEM((16, *square), BF16),
        pltpu.VMEM((16, 3, *square), BF16),
        pltpu.VMEM((16, *square), BF16),
        pltpu.VMEM((FEAT_ROWS, 4096), F32),
        pltpu.VMEM((2, BLOCK, FREQS), BF16),
        pltpu.VMEM((2, FREQS, BLOCK), BF16),
        pltpu.VMEM((3, *square), F32),
        pltpu.VMEM((128, 128), F32),
        pltpu.VMEM((BLOCK, 64), F32),
        pltpu.VMEM((BLOCK, 128), F32),
        pltpu.VMEM((BLOCK, 128), F32),
        pltpu.VMEM(square, F32),
        pltpu.VMEM((GROUP + BLOCK, FREQS), F32),
        pltpu.VMEM((BLOCK + LAG_PAD, BLOCK), F32),
        pltpu.VMEM((BLOCK + LAG_PAD, BLOCK), F32),
        pltpu.VMEM((BLOCK + LAG_PAD, BLOCK), F32),
        pltpu.VMEM((3, EDGE, BLOCK), BF16),
        pltpu.VMEM((3, EDGE, BLOCK), BF16),
        pltpu.VMEM((3, 16 + BLOCK, BLOCK), F32),
        pltpu.VMEM(square, F32),
        pltpu.VMEM(square, F32),
        pltpu.VMEM((BLOCKS, GROUP, BLOCK), BF16),
        pltpu.VMEM((BLOCKS, GROUP, BLOCK), BF16),
        pltpu.VMEM((LAG_PAD + BLOCK, FREQS), F32),
        pltpu.VMEM((BLOCK, FREQS), F32),
        pltpu.VMEM((BLOCKS, GROUP, BLOCK), BF16),
        pltpu.VMEM((BLOCKS, GROUP, BLOCK), BF16),
        pltpu.VMEM(square, BF16),
        pltpu.VMEM((16, *square), F32),
        pltpu.VMEM((2, 3, 128, BLOCK), BF16),
        pltpu.VMEM((2, 3, 128, BLOCK), BF16),
        pltpu.VMEM((2, 3, 3, 128, BLOCK), BF16),
        pltpu.VMEM((2, 3, 2, 64, BLOCK), BF16),
        pltpu.VMEM((2, 3, 2, 128, BLOCK), BF16),
        pltpu.VMEM((2, 3, 128, BLOCK), BF16),
        pltpu.VMEM((2, 3, 128, BLOCK), BF16),
        pltpu.VMEM((2, 128, BLOCK), F32),
        pltpu.SemaphoreType.REGULAR((3,)),
        dma((9,)),
        dma((16,)),
        dma((16,)),
        dma((44,)),
        dma((44,)),
        dma((1,)),
        dma((1,)),
        dma((16,)),
        dma((16,)),
        dma((16,)),
        dma((16,)),
        dma((36,)),
        dma((36,)),
    ]
    return pl.pallas_call(
        kernel,
        out_shape=jax.ShapeDtypeStruct(square, BF16),
        in_specs=[hbm] * 11,
        out_specs=vmem,
        scratch_shapes=scratch,
        compiler_params=pltpu.CompilerParams(
            collective_id=0, has_side_effects=True, vmem_limit_bytes=56 * 1024 * 1024
        ),
        name="hyena",
    )(
        tokens,
        jnp.transpose(in_weight, (1, 0, 2)),
        short_taps,
        filter_in,
        filter_out,
        rates.reshape(1, BLOCK),
        skip.reshape(1, BLOCK),
        out_weight,
        jnp.asarray(feats),
        jnp.asarray(forward),
        jnp.asarray(inverse),
    )


def solution(mesh):
    placed = (
        P("seq", "chan"),
        P(None, None, "chan"),
        P(None, None, "chan"),
        P(),
        P(None, "chan"),
        P("chan"),
        P("chan"),
        P("chan", None),
    )
    return jax.shard_map(
        per_device, mesh=mesh, in_specs=placed, out_specs=P("seq", "chan"), check_vma=False
    )
```

```python
import functools
import math

import jax
import jax.numpy as jnp
import ml_dtypes
import numpy as np
from jax import lax
from jax.experimental import pallas as pl
from jax.experimental.pallas import tpu as pltpu
from jax.sharding import PartitionSpec as P

BLOCK = 256
GROUP = 16
BLOCKS = 16
FREQS = 2 * BLOCK
FEAT_ROWS = 40
EDGE = 16
LAG_STEP = 4
LAG_PAD = (LAG_STEP - 1) * GROUP
ORDER = (8, 7, 9, 6, 10, 5, 11, 4, 12, 3, 13, 2, 14, 1, 15)
MESH_ID = pl.DeviceIdType.MESH
F32 = jnp.float32
BF16 = jnp.bfloat16


def split_two(values):
    high = values.astype(ml_dtypes.bfloat16)
    low = (values - high.astype(np.float64)).astype(ml_dtypes.bfloat16)
    return np.stack([high, low])


@functools.cache
def tables(total):
    row = np.arange(BLOCK)
    freq = np.arange(BLOCK)
    angle = 2.0 * np.pi * ((row[:, None] * freq[None, :]) % FREQS) / FREQS
    imag = -np.sin(angle)
    imag[:, 0] = 1.0 - 2.0 * (row % 2)
    forward = np.concatenate([np.cos(angle), imag], axis=1)
    angle = 2.0 * np.pi * ((freq[:, None] * (row[None, :] + BLOCK)) % FREQS) / FREQS
    real_rows = 2.0 * np.cos(angle)
    real_rows[0] = 1.0
    imag_rows = -2.0 * np.sin(angle)
    imag_rows[0] = 1.0 - 2.0 * (row % 2)
    inverse = np.concatenate([real_rows, imag_rows], axis=0) / FREQS
    place = np.arange(total)
    count = 16
    rates = 1 + np.arange(count) * (total // 4 - 1) // (count - 1)
    phase = (place[None, :] * rates[:, None]) % total
    turn = 2.0 * np.pi * phase / total
    feats = np.zeros((FEAT_ROWS, total), np.float32)
    feats[0] = place / total
    feats[1 : 1 + count] = np.cos(turn)
    feats[1 + count : 1 + 2 * count] = np.sin(turn)
    return split_two(forward), split_two(inverse), feats


def sine(x):
    turns = jnp.round(x * (1.0 / math.pi))
    r = x - turns * 3.140625
    r = r - turns * 0.0009670257568359375
    r = r - turns * 6.2771141529083252e-07
    odd = turns - 2.0 * jnp.floor(turns * 0.5)
    z = r * r
    poly = 1.0 / 6227020800.0
    for term in (-39916800.0, 362880.0, -5040.0, 120.0, -6.0):
        poly = poly * z + 1.0 / term
    value = r + r * z * poly
    return value * (1.0 - 2.0 * odd)


def dot(a, b):
    return jnp.dot(a, b, preferred_element_type=F32)


def halves(x):
    high = x.astype(BF16)
    return high, (x - high.astype(F32)).astype(BF16)


def slot(h, first, second):
    dx, dy = (first, second) if h == 0 else (second, first)
    return (dy % 4) * 4 + dx % 4


def rows(h, part):
    base = h * 128
    cut = EDGE if h else 0
    return {"f": (base, 128 - cut), "q1": (base, 64), "q2": (base + 64, 64 - cut)}[part]


class Links:
    def __init__(self, send, recv):
        self.send, self.recv, self.known = send, recv, {}

    def start(self, name, src, dst, device):
        index = len(self.known)
        copy = pltpu.make_async_remote_copy(
            src_ref=src,
            dst_ref=dst,
            send_sem=self.send.at[index],
            recv_sem=self.recv.at[index],
            device_id=device,
            device_id_type=MESH_ID,
        )
        copy.start()
        self.known[name] = copy

    def arrived(self, name):
        self.known[name].wait_recv()

    def finish(self):
        for copy in self.known.values():
            copy.wait_send()


def kernel(
    tok, win, taps_in, fin_in, fout_in, rates_in, skip_in, wout, feats, fmat, gmat,
    out,
    taps, fin, fout, rates, skip, xbuf, wbuf, wo, featbuf, fbuf, gbuf, acc, finp, fot, ratecol, skipcol, fs, aspec, sre, sim, sre2,
    edge_out, edge_in, pf, qbuf, drv, sbuf, dbuf, xs, ys, cbuf, rbuf, gated,
    part, snd, rq, rh, psnd, rp, red,
    word_sem, local_sem, w_sem, wo_sem, ag_send, ag_recv, halo_send, halo_recv, a_send, a_recv, b_send, b_recv, rs_send, rs_recv,
):
    s = lax.axis_index("seq")
    c = lax.axis_index("chan")
    x, y = lax.rem(c, 4), lax.div(c, 4)
    spots = [(dx, dy) for dy in range(4) for dx in range(4)]

    def chan_at(dx, dy):
        return lax.rem(y + dy + 4, 4) * 4 + lax.rem(x + dx + 4, 4)

    def neighbour(h, stage, sign):
        along_x = (h == 0) == (stage == 0)
        return {"chan": chan_at(sign, 0) if along_x else chan_at(0, sign)}

    z, core = lax.div(s, 2), lax.rem(s, 2)

    def plane(step):
        return {"seq": lax.rem(z + step + 8, 8) * 2 + core}

    sibling = {"seq": z * 2 + 1 - core}
    barrier = pltpu.get_barrier_semaphore()
    near = [{"chan": chan_at(step, 0)} for step in (1, -1, 2)]
    near += [{"chan": chan_at(0, step)} for step in (1, -1, 2)]
    near += [sibling, plane(1), plane(-1)]
    for device in near:
        pl.semaphore_signal(barrier, inc=1, device_id=device, device_id_type=MESH_ID)

    small = [
        pltpu.make_async_copy(src, dst, local_sem.at[4 + n])
        for n, (src, dst) in enumerate(
            ((fin_in, fin), (fout_in, fout), (rates_in, rates), (skip_in, skip), (taps_in, taps))
        )
    ]
    for copy in small:
        copy.start()
    own = pltpu.make_async_copy(tok, xbuf.at[0], local_sem.at[0])
    own.start()
    order = [(0, 0), (1, 0), (3, 0), (0, 1), (0, 3), (2, 0), (0, 2), (1, 1), (1, 3), (3, 1), (3, 3),
             (1, 2), (2, 1), (3, 2), (2, 3), (2, 2)]
    w_copies = {}
    feat_copy = pltpu.make_async_copy(feats, featbuf, local_sem.at[1])
    f_copy = pltpu.make_async_copy(fmat, fbuf, local_sem.at[2])
    g_copy = pltpu.make_async_copy(gmat, gbuf, local_sem.at[3])
    feat_copy.start()

    def start_weights(first, last):
        for n in range(first, last):
            dx, dy = order[n]
            at = pl.ds(pl.multiple_of(chan_at(-dx, -dy) * BLOCK, BLOCK), BLOCK)
            w_copies[dx, dy] = pltpu.make_async_copy(win.at[:, at, :], wbuf.at[n], w_sem.at[n])
            w_copies[dx, dy].start()

    start_weights(0, 1)
    wo_copies = {}

    pl.semaphore_wait(barrier, len(near))

    rounds = ([plane(1), plane(-1)], [plane(2), plane(-2)], [sibling])

    def tell(n):
        for device in rounds[n]:
            pl.semaphore_signal(word_sem.at[n], inc=1, device_id=device, device_id_type=MESH_ID)

    def hear(n):
        pl.semaphore_wait(word_sem.at[n], len(rounds[n]))

    links = Links(ag_send, ag_recv)

    def push(name, h, frm, to, piece, stage, sign):
        start, size = rows(h, piece)
        here = xbuf.at[slot(h, *frm), pl.ds(start, size), :]
        there = xbuf.at[slot(h, *to), pl.ds(start, size), :]
        links.start((name, h), here, there, neighbour(h, stage, sign))

    def take(*names):
        for name in names:
            for h in (0, 1):
                links.arrived((name, h))

    def multiply(blocks, first=False):
        for dx, dy in blocks:
            if (dx, dy) == (0, 0):
                w_copies[dx, dy].wait()
        for j in range(3):
            total = None if first else acc[j]
            for dx, dy in blocks:
                term = dot(xbuf[dy * 4 + dx], wbuf[order.index((dx, dy)), j])
                total = term if total is None else total + term
            acc[j] = total

    own.wait()
    tell(0)
    for h in (0, 1):
        push("P2", h, (0, 0), (2, 0), "f", 0, 2)
        push("P0+", h, (0, 0), (1, 0), "f", 0, 1)
        push("P0-", h, (0, 0), (3, 0), "f", 0, -1)
    for h in (0, 1):
        push("Q00+", h, (0, 0), (0, 1), "f", 1, 1)
        push("Q00-", h, (0, 0), (0, 3), "f", 1, -1)

    edge = pl.ds(BLOCK - EDGE, EDGE)
    for step in (1, 2, 3):
        links.start(
            ("EP", step),
            xbuf.at[0, edge, :],
            xbuf.at[step * (1 + 3 * core), edge, :],
            {"chan": chan_at(step * (1 - core), step * core)},
        )
    start_weights(1, 16)
    f_copy.start()

    for copy in small:
        copy.wait()
    finp[...] = jnp.zeros_like(finp)
    finp[0:33, 0:64] = fin[...]
    fin_t = jnp.transpose(finp[...])[0:64, 0:FEAT_ROWS]
    fot[...] = jnp.transpose(fout[...])
    ratecol[...] = jnp.transpose(jnp.broadcast_to(rates[...], (128, BLOCK)))
    skipcol[...] = jnp.transpose(jnp.broadcast_to(skip[...], (128, BLOCK)))
    mine = pl.ds(pl.multiple_of(s * GROUP, GROUP), GROUP)
    fo = fot[mine, :]
    rate = ratecol[mine, :]
    rate = jnp.concatenate([rate] * 4, axis=1)
    scale = jnp.sqrt(rate)
    feat_copy.wait()

    def filter_piece(n, carry):
        at = pl.ds(pl.multiple_of(n * 512, 512), 512)
        arg = jnp.dot(fin_t, featbuf[:, at], precision=lax.Precision.HIGHEST, preferred_element_type=F32)
        shaped = jnp.dot(fo, sine(arg), precision=lax.Precision.HIGHEST, preferred_element_type=F32)
        place = (lax.broadcasted_iota(jnp.int32, (GROUP, 512), 1) + n * 512).astype(F32)
        value = shaped * scale * jnp.exp(-rate * place)
        fs[pl.ds(pl.multiple_of(n * 32, 32), GROUP), :] = value[:, :BLOCK]
        fs[pl.ds(pl.multiple_of(n * 32 + 16, 16), GROUP), :] = value[:, BLOCK:]
        return carry

    lax.fori_loop(0, 4, filter_piece, 0)
    multiply([(0, 0)], first=True)

    take("P0+", "P0-")
    for h in (0, 1):
        for dp in (1, 3):
            push(f"Q{dp}0+", h, (dp, 0), (dp, 1), "f", 1, 1)
            push(f"Q{dp}0-", h, (dp, 0), (dp, 3), "f", 1, -1)
    take("P2")
    for h in (0, 1):
        push("Q20+", h, (2, 0), (2, 1), "f", 1, 1)
        push("Q20-", h, (2, 0), (2, 3), "f", 1, -1)
    take("Q00+", "Q00-")
    for h in (0, 1):
        push("Q01+", h, (0, 1), (0, 2), "q1", 1, 1)
        push("Q01-", h, (0, 3), (0, 2), "q2", 1, -1)
    for step in (1, 2, 3):
        links.arrived(("EP", step))
    for step in (1, 2, 3):
        for k in range(4):
            links.start(
                ("EQ", step, k),
                xbuf.at[k * (1 + 3 * core), edge, :],
                xbuf.at[k * (1 + 3 * core) + step * (4 - 3 * core), edge, :],
                {"chan": chan_at(step * core, step * (1 - core))},
            )
    hear(0)
    tell(1)
    lax.fori_loop(4, 8, filter_piece, 0)
    for dp in (1, 3):
        take(f"Q{dp}0+", f"Q{dp}0-")
        for h in (0, 1):
            push(f"Q{dp}1+", h, (dp, 1), (dp, 2), "q1", 1, 1)
            push(f"Q{dp}1-", h, (dp, 3), (dp, 2), "q2", 1, -1)

    take("Q20+", "Q20-")
    for h in (0, 1):
        push("Q21+", h, (2, 1), (2, 2), "q1", 1, 1)
        push("Q21-", h, (2, 3), (2, 2), "q2", 1, -1)

    for step in (1, 2, 3):
        for k in range(4):
            links.arrived(("EQ", step, k))
    for dx, dy in order[1:]:
        w_copies[dx, dy].wait()
    for j in range(3):
        total = None
        for dx, dy in order:
            term = dot(xbuf[dy * 4 + dx, BLOCK - EDGE :, :], wbuf[order.index((dx, dy)), j])
            total = term if total is None else total + term
        edge_out[j] = total.astype(BF16)
    halo = pltpu.make_async_remote_copy(
        src_ref=edge_out,
        dst_ref=edge_in,
        send_sem=halo_send.at[0],
        recv_sem=halo_recv.at[0],
        device_id={"seq": lax.rem(s + 1, BLOCKS)},
        device_id_type=MESH_ID,
    )
    halo.start()
    hear(1)
    tell(2)
    g_copy.start()
    for n, (dx, dy) in enumerate(spots):
        at = pl.ds(pl.multiple_of(chan_at(dx, dy) * BLOCK, BLOCK), BLOCK)
        wo_copies[dx, dy] = pltpu.make_async_copy(wout.at[:, at], wo.at[n], wo_sem.at[n])
        wo_copies[dx, dy].start()

    take("Q01+", "Q01-")
    multiply(order[1:11])
    for h, dp, block in ((0, 1, (1, 2)), (1, 1, (2, 1)), (0, 3, (3, 2)), (1, 3, (2, 3))):
        links.arrived((f"Q{dp}1+", h))
        links.arrived((f"Q{dp}1-", h))
        multiply([block])
    hear(2)
    take("Q21+", "Q21-")
    multiply([(2, 2)])

    for j in range(3):
        pf[j, 16:, :] = acc[j].astype(BF16).astype(F32)

    def short(start, size):
        branch = []
        for j in range(3):
            value = taps[0, pl.ds(j, 1), :] * pf[j, pl.ds(16 + start, size), :]
            value = value + taps[1, pl.ds(j, 1), :] * pf[j, pl.ds(15 + start, size), :]
            branch.append(value + taps[2, pl.ds(j, 1), :] * pf[j, pl.ds(14 + start, size), :])
        qbuf[pl.ds(start, size), :] = branch[0]
        drv[pl.ds(start, size), :] = branch[1] * branch[2]

    halo.wait_recv()
    live = (s > 0).astype(F32)
    for j in range(3):
        pf[j, 0:16, :] = edge_in[j].astype(F32) * live
    for start in range(0, BLOCK, 32):
        short(start, 32)

    sbuf[...] = jnp.transpose(drv[...]).astype(BF16).reshape(BLOCKS, GROUP, BLOCK)

    def give(k, src, dst, send, recv):
        other = lax.rem(s + k, BLOCKS)
        copy = pltpu.make_async_remote_copy(
            src_ref=src,
            dst_ref=dst.at[s],
            send_sem=send.at[k],
            recv_sem=recv.at[k],
            device_id={"seq": other},
            device_id_type=MESH_ID,
        )
        copy.start()
        return copy

    gone = [give(k, sbuf.at[lax.rem(s + k, BLOCKS)], dbuf, a_send, a_recv) for k in ORDER]
    dbuf[pl.ds(s, 1)] = sbuf[pl.ds(s, 1)]
    f_copy.wait()
    high, low = halves(fs[...])
    aspec[0:GROUP, :] = jnp.zeros((GROUP, FREQS), F32)
    aspec[GROUP:, :] = dot(high, fbuf[0]) + dot(low, fbuf[0]) + dot(high, fbuf[1])
    lane = lax.broadcasted_iota(jnp.int32, (GROUP, BLOCK), 1)
    parity = 1.0 - 2.0 * lax.rem(lane, 2).astype(F32)

    for table in (sre, sim, sre2):
        table[BLOCK:, :] = jnp.zeros((LAG_PAD, BLOCK), F32)

    def lag_piece(n, carry):
        before = pl.ds(pl.multiple_of(n * GROUP, GROUP), GROUP)
        after = pl.ds(pl.multiple_of(n * GROUP + GROUP, GROUP), GROUP)
        re = aspec[before, 0:BLOCK] + parity * aspec[after, 0:BLOCK]
        im = aspec[before, BLOCK:] + parity * aspec[after, BLOCK:]
        sre[before, :] = re
        sim[before, :] = jnp.where(lane == 0, 0.0, im)
        sre2[before, :] = jnp.where(lane == 0, im, re)
        return carry

    lax.fori_loop(0, BLOCKS, lag_piece, 0)

    xs[0:LAG_PAD, :] = jnp.zeros((LAG_PAD, FREQS), F32)
    direct = skipcol[mine, :]
    direct = jnp.concatenate([direct, direct], axis=1)
    g_copy.wait()
    for copy in gone:
        copy.wait_recv()
    waits = [halo] + gone

    drive = dbuf[...].reshape(BLOCK, BLOCK)
    xs[LAG_PAD:, :] = dot(drive, fbuf[0]) + dot(drive, fbuf[1])

    def spectrum(n, i):
        def lags(turn, total):
            re, im = total
            for d in range(LAG_STEP):
                d = turn * LAG_STEP + d
                at = pl.ds(pl.multiple_of((i - d) * GROUP + LAG_PAD, GROUP), GROUP)
                by = pl.ds(pl.multiple_of(d * GROUP, GROUP), GROUP)
                xr, xi = xs[at, 0:BLOCK], xs[at, BLOCK:]
                part_im = sim[by, :]
                re = re + (xr * sre[by, :] - xi * part_im)
                im = im + (xr * part_im + xi * sre2[by, :])
            return re, im

        zero = jnp.zeros((GROUP, BLOCK), F32)
        re, im = lax.fori_loop(0, lax.div(i + LAG_STEP, LAG_STEP), lags, (zero, zero))
        ys[n * GROUP : (n + 1) * GROUP, 0:BLOCK] = re
        ys[n * GROUP : (n + 1) * GROUP, BLOCK:] = im

    steps = ORDER + (0,)
    for start in (0, 8):
        for n in range(start, start + 8):
            spectrum(n, lax.rem(s + steps[n], BLOCKS))
        some = slice(start * GROUP, start * GROUP + 8 * GROUP)
        high, low = halves(ys[some, :])
        both = dot(jnp.concatenate([high, low], axis=0), gbuf[0])
        conv = both[: 8 * GROUP] + both[8 * GROUP :] + dot(high, gbuf[1])
        for n in range(start, start + 8):
            i = lax.rem(s + steps[n], BLOCKS)
            value = conv[(n - start) * GROUP : (n - start + 1) * GROUP, :]
            cbuf[n] = (value + direct * dbuf[i].astype(F32)).astype(BF16)
            if steps[n]:
                waits.append(give(steps[n], cbuf.at[n], rbuf, b_send, b_recv))
    rbuf[pl.ds(s, 1)] = cbuf[pl.ds(BLOCKS - 1, 1)]
    for copy in waits[-15:]:
        copy.wait_recv()

    back = jnp.transpose(rbuf[...].reshape(BLOCK, BLOCK).astype(F32))
    gated[...] = (qbuf[...] * back).astype(BF16)

    sums = Links(rs_send, rs_recv)

    def project(dx, dy):
        wo_copies[dx, dy].wait()
        part[dy * 4 + dx] = dot(gated[...], wo[dy * 4 + dx])

    def half(h, dp, dq):
        return part.at[slot(h, dp, dq), pl.ds(h * 128, 128), :]

    column = (2, 1, 3, 0)

    def relay(h, e):
        snd[h, e, 0] = half(h, column[e], 2)[...].astype(BF16)
        sums.start(("Q1+", h, e), snd.at[h, e, 0, pl.ds(0, 64), :], rq.at[h, e, 0], neighbour(h, 1, 1))
        sums.start(("Q1-", h, e), snd.at[h, e, 0, pl.ds(64, 64), :], rq.at[h, e, 1], neighbour(h, 1, -1))

    for e in range(4):
        for h in (0, 1):
            if e or not h:
                project(*((column[e], 2) if h == 0 else (2, column[e])))
            relay(h, e)
    for dx, dy in ((1, 1), (1, 3), (3, 1), (3, 3), (0, 1), (1, 0), (0, 3), (3, 0), (0, 0)):
        project(dx, dy)

    for e in range(4):
        for h in (0, 1):
            sums.arrived(("Q1+", h, e))
            one = half(h, column[e], 1)
            snd[h, e, 1, 0:64] = (one[0:64, :] + rq[h, e, 0].astype(F32)).astype(BF16)
            snd[h, e, 1, 64:128] = one[64:128, :].astype(BF16)
            sums.start(("Q2+", h, e), snd.at[h, e, 1], rh.at[h, e, 0], neighbour(h, 1, 1))
            sums.arrived(("Q1-", h, e))
            one = half(h, column[e], 3)
            snd[h, e, 2, 0:64] = one[0:64, :].astype(BF16)
            snd[h, e, 2, 64:128] = (one[64:128, :] + rq[h, e, 1].astype(F32)).astype(BF16)
            sums.start(("Q2-", h, e), snd.at[h, e, 2], rh.at[h, e, 1], neighbour(h, 1, -1))

    def reduced(h, e):
        sums.arrived(("Q2+", h, e))
        sums.arrived(("Q2-", h, e))
        return half(h, column[e], 0)[...] + rh[h, e, 0].astype(F32) + rh[h, e, 1].astype(F32)

    for e, sign in ((0, 2), (1, 1), (2, -1)):
        for h in (0, 1):
            psnd[h, e] = reduced(h, e).astype(BF16)
            sums.start(("P", h, e), psnd.at[h, e], rp.at[h, e], neighbour(h, 0, sign))
    for h in (0, 1):
        red[h] = reduced(h, 3)
    for h in (0, 1):
        total = red[h]
        for n in (0, 1, 2):
            sums.arrived(("P", h, n))
            total = total + rp[h, n].astype(F32)
        out[h * 128 : h * 128 + 128, :] = total.astype(BF16)

    links.finish()
    sums.finish()
    for copy in waits:
        copy.wait_send()


def per_device(tokens, in_weight, short_taps, filter_in, filter_out, rates, skip, out_weight):
    forward, inverse, feats = tables(4096)
    vmem = pl.BlockSpec(memory_space=pltpu.VMEM)
    hbm = pl.BlockSpec(memory_space=pl.ANY)
    dma = pltpu.SemaphoreType.DMA
    square = (BLOCK, BLOCK)
    scratch = [
        pltpu.VMEM((3, 3, BLOCK), F32),
        pltpu.VMEM((33, 64), F32),
        pltpu.VMEM((64, BLOCK), F32),
        pltpu.VMEM((1, BLOCK), F32),
        pltpu.VMEM((1, BLOCK), F32),
        pltpu.VMEM((16, *square), BF16),
        pltpu.VMEM((16, 3, *square), BF16),
        pltpu.VMEM((16, *square), BF16),
        pltpu.VMEM((FEAT_ROWS, 4096), F32),
        pltpu.VMEM((2, BLOCK, FREQS), BF16),
        pltpu.VMEM((2, FREQS, BLOCK), BF16),
        pltpu.VMEM((3, *square), F32),
        pltpu.VMEM((128, 128), F32),
        pltpu.VMEM((BLOCK, 64), F32),
        pltpu.VMEM((BLOCK, 128), F32),
        pltpu.VMEM((BLOCK, 128), F32),
        pltpu.VMEM(square, F32),
        pltpu.VMEM((GROUP + BLOCK, FREQS), F32),
        pltpu.VMEM((BLOCK + LAG_PAD, BLOCK), F32),
        pltpu.VMEM((BLOCK + LAG_PAD, BLOCK), F32),
        pltpu.VMEM((BLOCK + LAG_PAD, BLOCK), F32),
        pltpu.VMEM((3, EDGE, BLOCK), BF16),
        pltpu.VMEM((3, EDGE, BLOCK), BF16),
        pltpu.VMEM((3, 16 + BLOCK, BLOCK), F32),
        pltpu.VMEM(square, F32),
        pltpu.VMEM(square, F32),
        pltpu.VMEM((BLOCKS, GROUP, BLOCK), BF16),
        pltpu.VMEM((BLOCKS, GROUP, BLOCK), BF16),
        pltpu.VMEM((LAG_PAD + BLOCK, FREQS), F32),
        pltpu.VMEM((BLOCK, FREQS), F32),
        pltpu.VMEM((BLOCKS, GROUP, BLOCK), BF16),
        pltpu.VMEM((BLOCKS, GROUP, BLOCK), BF16),
        pltpu.VMEM(square, BF16),
        pltpu.VMEM((16, *square), F32),
        pltpu.VMEM((2, 4, 3, 128, BLOCK), BF16),
        pltpu.VMEM((2, 4, 2, 64, BLOCK), BF16),
        pltpu.VMEM((2, 4, 2, 128, BLOCK), BF16),
        pltpu.VMEM((2, 3, 128, BLOCK), BF16),
        pltpu.VMEM((2, 3, 128, BLOCK), BF16),
        pltpu.VMEM((2, 128, BLOCK), F32),
        pltpu.SemaphoreType.REGULAR((3,)),
        dma((9,)),
        dma((16,)),
        dma((16,)),
        dma((53,)),
        dma((53,)),
        dma((1,)),
        dma((1,)),
        dma((16,)),
        dma((16,)),
        dma((16,)),
        dma((16,)),
        dma((38,)),
        dma((38,)),
    ]
    return pl.pallas_call(
        kernel,
        out_shape=pltpu.VMEM(square, BF16),
        in_specs=[hbm] * 11,
        out_specs=vmem,
        scratch_shapes=scratch,
        compiler_params=pltpu.CompilerParams(
            collective_id=0, has_side_effects=True, vmem_limit_bytes=56 * 1024 * 1024
        ),
        name="hyena",
    )(
        tokens,
        jnp.transpose(in_weight, (1, 0, 2)),
        short_taps,
        filter_in,
        filter_out,
        rates.reshape(1, BLOCK),
        skip.reshape(1, BLOCK),
        out_weight,
        jnp.asarray(feats),
        jnp.asarray(forward),
        jnp.asarray(inverse),
    )


def solution(mesh):
    placed = (
        P("seq", "chan"),
        P(None, None, "chan"),
        P(None, None, "chan"),
        P(),
        P(None, "chan"),
        P("chan"),
        P("chan"),
        P("chan", None),
    )
    return jax.shard_map(
        per_device, mesh=mesh, in_specs=placed, out_specs=P("seq", "chan"), check_vma=False
    )
```

```python
import functools
import math

import jax
import jax.numpy as jnp
import ml_dtypes
import numpy as np
from jax import lax
from jax.experimental import pallas as pl
from jax.experimental.pallas import tpu as pltpu
from jax.sharding import PartitionSpec as P

BLOCK = 256
GROUP = 16
BLOCKS = 16
FREQS = 2 * BLOCK
FEAT_ROWS = 40
EDGE = 16
LAG_STEP = 4
LAG_PAD = (LAG_STEP - 1) * GROUP
ORDER = (8, 7, 9, 6, 10, 5, 11, 4, 12, 3, 13, 2, 14, 1, 15)
MESH_ID = pl.DeviceIdType.MESH
F32 = jnp.float32
BF16 = jnp.bfloat16


def split_two(values):
    high = values.astype(ml_dtypes.bfloat16)
    low = (values - high.astype(np.float64)).astype(ml_dtypes.bfloat16)
    return np.stack([high, low])


@functools.cache
def tables(total):
    row = np.arange(BLOCK)
    freq = np.arange(BLOCK)
    angle = 2.0 * np.pi * ((row[:, None] * freq[None, :]) % FREQS) / FREQS
    imag = -np.sin(angle)
    imag[:, 0] = 1.0 - 2.0 * (row % 2)
    forward = np.concatenate([np.cos(angle), imag], axis=1)
    angle = 2.0 * np.pi * ((freq[:, None] * (row[None, :] + BLOCK)) % FREQS) / FREQS
    real_rows = 2.0 * np.cos(angle)
    real_rows[0] = 1.0
    imag_rows = -2.0 * np.sin(angle)
    imag_rows[0] = 1.0 - 2.0 * (row % 2)
    inverse = np.concatenate([real_rows, imag_rows], axis=0) / FREQS
    place = np.arange(total)
    count = 16
    rates = 1 + np.arange(count) * (total // 4 - 1) // (count - 1)
    phase = (place[None, :] * rates[:, None]) % total
    turn = 2.0 * np.pi * phase / total
    feats = np.zeros((FEAT_ROWS, total), np.float32)
    feats[0] = place / total
    feats[1 : 1 + count] = np.cos(turn)
    feats[1 + count : 1 + 2 * count] = np.sin(turn)
    return split_two(forward), split_two(inverse), feats


def sine(x):
    turns = jnp.round(x * (1.0 / math.pi))
    r = x - turns * 3.140625
    r = r - turns * 0.0009670257568359375
    r = r - turns * 6.2771141529083252e-07
    odd = turns - 2.0 * jnp.floor(turns * 0.5)
    z = r * r
    poly = 1.0 / 6227020800.0
    for term in (-39916800.0, 362880.0, -5040.0, 120.0, -6.0):
        poly = poly * z + 1.0 / term
    value = r + r * z * poly
    return value * (1.0 - 2.0 * odd)


def dot(a, b):
    return jnp.dot(a, b, preferred_element_type=F32)


def halves(x):
    high = x.astype(BF16)
    return high, (x - high.astype(F32)).astype(BF16)


def slot(h, first, second):
    dx, dy = (first, second) if h == 0 else (second, first)
    return (dy % 4) * 4 + dx % 4


def rows(h, part):
    base = h * 128
    cut = EDGE if h else 0
    return {"f": (base, 128 - cut), "q1": (base, 64), "q2": (base + 64, 64 - cut)}[part]


class Links:
    def __init__(self, send, recv):
        self.send, self.recv, self.known = send, recv, {}

    def start(self, name, src, dst, device):
        index = len(self.known)
        copy = pltpu.make_async_remote_copy(
            src_ref=src,
            dst_ref=dst,
            send_sem=self.send.at[index],
            recv_sem=self.recv.at[index],
            device_id=device,
            device_id_type=MESH_ID,
        )
        copy.start()
        self.known[name] = copy

    def arrived(self, name):
        self.known[name].wait_recv()

    def finish(self):
        for copy in self.known.values():
            copy.wait_send()


def kernel(
    tok, win, taps_in, fin_in, fout_in, rates_in, skip_in, wout, feats, fmat, gmat,
    out,
    taps, fin, fout, rates, skip, xbuf, wbuf, wo, featbuf, fbuf, gbuf, acc, finp, fot, ratecol, skipcol, fs, aspec, sre, sim, sre2,
    edge_out, edge_in, pf, qbuf, drv, sbuf, dbuf, xs, ys, cbuf, rbuf, gated,
    part, snd, rq, rh, psnd, rp, red,
    word_sem, local_sem, w_sem, wo_sem, ag_send, ag_recv, halo_send, halo_recv, a_send, a_recv, b_send, b_recv, rs_send, rs_recv,
):
    s = lax.axis_index("seq")
    c = lax.axis_index("chan")
    x, y = lax.rem(c, 4), lax.div(c, 4)
    spots = [(dx, dy) for dy in range(4) for dx in range(4)]

    def chan_at(dx, dy):
        return lax.rem(y + dy + 4, 4) * 4 + lax.rem(x + dx + 4, 4)

    def neighbour(h, stage, sign):
        along_x = (h == 0) == (stage == 0)
        return {"chan": chan_at(sign, 0) if along_x else chan_at(0, sign)}

    z, core = lax.div(s, 2), lax.rem(s, 2)

    def plane(step):
        return {"seq": lax.rem(z + step + 8, 8) * 2 + core}

    sibling = {"seq": z * 2 + 1 - core}
    barrier = pltpu.get_barrier_semaphore()
    near = [{"chan": chan_at(step, 0)} for step in (1, -1, 2)]
    near += [{"chan": chan_at(0, step)} for step in (1, -1, 2)]
    near += [sibling, plane(1), plane(-1)]
    for device in near:
        pl.semaphore_signal(barrier, inc=1, device_id=device, device_id_type=MESH_ID)

    small = [
        pltpu.make_async_copy(src, dst, local_sem.at[4 + n])
        for n, (src, dst) in enumerate(
            ((fin_in, fin), (fout_in, fout), (rates_in, rates), (skip_in, skip), (taps_in, taps))
        )
    ]
    for copy in small:
        copy.start()
    own = pltpu.make_async_copy(tok, xbuf.at[0], local_sem.at[0])
    own.start()
    order = [(0, 0), (1, 0), (3, 0), (0, 1), (0, 3), (2, 0), (0, 2), (1, 1), (1, 3), (3, 1), (3, 3),
             (1, 2), (2, 1), (3, 2), (2, 3), (2, 2)]
    w_copies = {}
    feat_copy = pltpu.make_async_copy(feats, featbuf, local_sem.at[1])
    f_copy = pltpu.make_async_copy(fmat, fbuf, local_sem.at[2])
    g_copy = pltpu.make_async_copy(gmat, gbuf, local_sem.at[3])
    feat_copy.start()

    def start_weights(first, last):
        for n in range(first, last):
            dx, dy = order[n]
            at = pl.ds(pl.multiple_of(chan_at(-dx, -dy) * BLOCK, BLOCK), BLOCK)
            w_copies[dx, dy] = pltpu.make_async_copy(win.at[:, at, :], wbuf.at[n], w_sem.at[n])
            w_copies[dx, dy].start()

    start_weights(0, 1)
    wo_copies = {}

    pl.semaphore_wait(barrier, len(near))

    rounds = ([plane(1), plane(-1)], [plane(2), plane(-2)], [sibling])

    def tell(n):
        for device in rounds[n]:
            pl.semaphore_signal(word_sem.at[n], inc=1, device_id=device, device_id_type=MESH_ID)

    def hear(n):
        pl.semaphore_wait(word_sem.at[n], len(rounds[n]))

    links = Links(ag_send, ag_recv)

    def push(name, h, frm, to, piece, stage, sign):
        start, size = rows(h, piece)
        here = xbuf.at[slot(h, *frm), pl.ds(start, size), :]
        there = xbuf.at[slot(h, *to), pl.ds(start, size), :]
        links.start((name, h), here, there, neighbour(h, stage, sign))

    def take(*names):
        for name in names:
            for h in (0, 1):
                links.arrived((name, h))

    def multiply(blocks, first=False):
        for dx, dy in blocks:
            if (dx, dy) == (0, 0):
                w_copies[dx, dy].wait()
        for j in range(3):
            total = None if first else acc[j]
            for dx, dy in blocks:
                term = dot(xbuf[dy * 4 + dx], wbuf[order.index((dx, dy)), j])
                total = term if total is None else total + term
            acc[j] = total

    own.wait()
    tell(0)
    for h in (0, 1):
        push("P2", h, (0, 0), (2, 0), "f", 0, 2)
        push("P0+", h, (0, 0), (1, 0), "f", 0, 1)
        push("P0-", h, (0, 0), (3, 0), "f", 0, -1)
    for h in (0, 1):
        push("Q00+", h, (0, 0), (0, 1), "f", 1, 1)
        push("Q00-", h, (0, 0), (0, 3), "f", 1, -1)

    edge = pl.ds(BLOCK - EDGE, EDGE)
    for step in (1, 2, 3):
        links.start(
            ("EP", step),
            xbuf.at[0, edge, :],
            xbuf.at[step * (1 + 3 * core), edge, :],
            {"chan": chan_at(step * (1 - core), step * core)},
        )
    start_weights(1, 16)
    f_copy.start()

    for copy in small:
        copy.wait()
    finp[...] = jnp.zeros_like(finp)
    finp[0:33, 0:64] = fin[...]
    fin_t = jnp.transpose(finp[...])[0:64, 0:FEAT_ROWS]
    fot[...] = jnp.transpose(fout[...])
    ratecol[...] = jnp.transpose(jnp.broadcast_to(rates[...], (128, BLOCK)))
    skipcol[...] = jnp.transpose(jnp.broadcast_to(skip[...], (128, BLOCK)))
    mine = pl.ds(pl.multiple_of(s * GROUP, GROUP), GROUP)
    fo = fot[mine, :]
    rate = ratecol[mine, :]
    rate = jnp.concatenate([rate] * 4, axis=1)
    scale = jnp.sqrt(rate)
    feat_copy.wait()

    def filter_piece(n, carry):
        at = pl.ds(pl.multiple_of(n * 512, 512), 512)
        arg = jnp.dot(fin_t, featbuf[:, at], precision=lax.Precision.HIGHEST, preferred_element_type=F32)
        shaped = jnp.dot(fo, sine(arg), precision=lax.Precision.HIGHEST, preferred_element_type=F32)
        place = (lax.broadcasted_iota(jnp.int32, (GROUP, 512), 1) + n * 512).astype(F32)
        value = shaped * scale * jnp.exp(-rate * place)
        fs[pl.ds(pl.multiple_of(n * 32, 32), GROUP), :] = value[:, :BLOCK]
        fs[pl.ds(pl.multiple_of(n * 32 + 16, 16), GROUP), :] = value[:, BLOCK:]
        return carry

    lax.fori_loop(0, 4, filter_piece, 0)
    multiply([(0, 0)], first=True)

    take("P0+", "P0-")
    for h in (0, 1):
        for dp in (1, 3):
            push(f"Q{dp}0+", h, (dp, 0), (dp, 1), "f", 1, 1)
            push(f"Q{dp}0-", h, (dp, 0), (dp, 3), "f", 1, -1)
    take("P2")
    for h in (0, 1):
        push("Q20+", h, (2, 0), (2, 1), "f", 1, 1)
        push("Q20-", h, (2, 0), (2, 3), "f", 1, -1)
    take("Q00+", "Q00-")
    for h in (0, 1):
        push("Q01+", h, (0, 1), (0, 2), "q1", 1, 1)
        push("Q01-", h, (0, 3), (0, 2), "q2", 1, -1)
    for step in (1, 2, 3):
        links.arrived(("EP", step))
    for step in (1, 2, 3):
        for k in range(4):
            links.start(
                ("EQ", step, k),
                xbuf.at[k * (1 + 3 * core), edge, :],
                xbuf.at[k * (1 + 3 * core) + step * (4 - 3 * core), edge, :],
                {"chan": chan_at(step * core, step * (1 - core))},
            )
    hear(0)
    tell(1)
    lax.fori_loop(4, 8, filter_piece, 0)
    for dp in (1, 3):
        take(f"Q{dp}0+", f"Q{dp}0-")
        for h in (0, 1):
            push(f"Q{dp}1+", h, (dp, 1), (dp, 2), "q1", 1, 1)
            push(f"Q{dp}1-", h, (dp, 3), (dp, 2), "q2", 1, -1)

    take("Q20+", "Q20-")
    for h in (0, 1):
        push("Q21+", h, (2, 1), (2, 2), "q1", 1, 1)
        push("Q21-", h, (2, 3), (2, 2), "q2", 1, -1)

    for step in (1, 2, 3):
        for k in range(4):
            links.arrived(("EQ", step, k))
    for dx, dy in order[1:]:
        w_copies[dx, dy].wait()
    for j in range(3):
        total = None
        for dx, dy in order:
            term = dot(xbuf[dy * 4 + dx, BLOCK - EDGE :, :], wbuf[order.index((dx, dy)), j])
            total = term if total is None else total + term
        edge_out[j] = total.astype(BF16)
    halo = pltpu.make_async_remote_copy(
        src_ref=edge_out,
        dst_ref=edge_in,
        send_sem=halo_send.at[0],
        recv_sem=halo_recv.at[0],
        device_id={"seq": lax.rem(s + 1, BLOCKS)},
        device_id_type=MESH_ID,
    )
    halo.start()
    hear(1)
    tell(2)
    g_copy.start()
    for n, (dx, dy) in enumerate(spots):
        at = pl.ds(pl.multiple_of(chan_at(dx, dy) * BLOCK, BLOCK), BLOCK)
        wo_copies[dx, dy] = pltpu.make_async_copy(wout.at[:, at], wo.at[n], wo_sem.at[n])
        wo_copies[dx, dy].start()

    f_copy.wait()
    high, low = halves(fs[...])
    aspec[0:GROUP, :] = jnp.zeros((GROUP, FREQS), F32)
    aspec[GROUP:, :] = dot(high, fbuf[0]) + dot(low, fbuf[0]) + dot(high, fbuf[1])
    lane = lax.broadcasted_iota(jnp.int32, (GROUP, BLOCK), 1)
    parity = 1.0 - 2.0 * lax.rem(lane, 2).astype(F32)

    for table in (sre, sim, sre2):
        table[BLOCK:, :] = jnp.zeros((LAG_PAD, BLOCK), F32)

    def lag_piece(n, carry):
        before = pl.ds(pl.multiple_of(n * GROUP, GROUP), GROUP)
        after = pl.ds(pl.multiple_of(n * GROUP + GROUP, GROUP), GROUP)
        re = aspec[before, 0:BLOCK] + parity * aspec[after, 0:BLOCK]
        im = aspec[before, BLOCK:] + parity * aspec[after, BLOCK:]
        sre[before, :] = re
        sim[before, :] = jnp.where(lane == 0, 0.0, im)
        sre2[before, :] = jnp.where(lane == 0, im, re)
        return carry

    lax.fori_loop(0, BLOCKS, lag_piece, 0)

    take("Q01+", "Q01-")
    multiply(order[1:11])
    for h, dp, block in ((0, 1, (1, 2)), (1, 1, (2, 1)), (0, 3, (3, 2)), (1, 3, (2, 3))):
        links.arrived((f"Q{dp}1+", h))
        links.arrived((f"Q{dp}1-", h))
        multiply([block])
    hear(2)
    take("Q21+", "Q21-")
    multiply([(2, 2)])

    for j in range(3):
        pf[j, 16:, :] = acc[j].astype(BF16).astype(F32)

    def short(start, size):
        branch = []
        for j in range(3):
            value = taps[0, pl.ds(j, 1), :] * pf[j, pl.ds(16 + start, size), :]
            value = value + taps[1, pl.ds(j, 1), :] * pf[j, pl.ds(15 + start, size), :]
            branch.append(value + taps[2, pl.ds(j, 1), :] * pf[j, pl.ds(14 + start, size), :])
        qbuf[pl.ds(start, size), :] = branch[0]
        drv[pl.ds(start, size), :] = branch[1] * branch[2]

    halo.wait_recv()
    live = (s > 0).astype(F32)
    for j in range(3):
        pf[j, 0:16, :] = edge_in[j].astype(F32) * live
    for start in range(0, BLOCK, 32):
        short(start, 32)

    sbuf[...] = jnp.transpose(drv[...]).astype(BF16).reshape(BLOCKS, GROUP, BLOCK)

    def message(src, dst, send, recv, other):
        return pltpu.make_async_remote_copy(
            src_ref=src,
            dst_ref=dst.at[s],
            send_sem=send,
            recv_sem=recv.at[s],
            device_id={"seq": other},
            device_id_type=MESH_ID,
        )

    def got(j, buffer, send, recv):
        @pl.when(s != j)
        def _():
            pltpu.make_async_remote_copy(
                src_ref=buffer.at[j],
                dst_ref=buffer.at[j],
                send_sem=send.at[0],
                recv_sem=recv.at[j],
                device_id={"seq": lax.rem(s + 1, BLOCKS)},
                device_id_type=MESH_ID,
            ).wait_recv()

    waits = [halo]
    for k in ORDER:
        other = lax.rem(s + k, BLOCKS)
        copy = message(sbuf.at[other], dbuf, a_send.at[k], a_recv, other)
        copy.start()
        waits.append(copy)
    dbuf[pl.ds(s, 1)] = sbuf[pl.ds(s, 1)]
    xs[0:LAG_PAD, :] = jnp.zeros((LAG_PAD, FREQS), F32)
    direct = skipcol[mine, :]
    direct = jnp.concatenate([direct, direct], axis=1)
    g_copy.wait()

    def spectrum(i):
        def lags(turn, total):
            re, im = total
            for d in range(LAG_STEP):
                d = turn * LAG_STEP + d
                at = pl.ds(pl.multiple_of((i - d) * GROUP + LAG_PAD, GROUP), GROUP)
                by = pl.ds(pl.multiple_of(d * GROUP, GROUP), GROUP)
                xr, xi = xs[at, 0:BLOCK], xs[at, BLOCK:]
                part_im = sim[by, :]
                re = re + (xr * sre[by, :] - xi * part_im)
                im = im + (xr * part_im + xi * sre2[by, :])
            return re, im

        zero = jnp.zeros((GROUP, BLOCK), F32)
        re, im = lax.fori_loop(0, (i + LAG_STEP) // LAG_STEP, lags, (zero, zero))
        ys[i * GROUP : (i + 1) * GROUP, 0:BLOCK] = re
        ys[i * GROUP : (i + 1) * GROUP, BLOCK:] = im

    returns = []
    for low_block, high_block in ((0, 4), (4, 8), (8, 16)):
        count = (high_block - low_block) * GROUP
        for j in range(low_block, high_block):
            got(j, dbuf, a_send, a_recv)
        some = slice(low_block * GROUP, high_block * GROUP)
        drive = dbuf[low_block:high_block].reshape(count, BLOCK)
        xs[LAG_PAD + some.start : LAG_PAD + some.stop, :] = dot(drive, fbuf[0]) + dot(drive, fbuf[1])
        for i in range(low_block, high_block):
            spectrum(i)
        high, low = halves(ys[some, :])
        both = dot(jnp.concatenate([high, low], axis=0), gbuf[0])
        conv = both[:count] + both[count:] + dot(high, gbuf[1])
        for i in range(low_block, high_block):
            value = conv[(i - low_block) * GROUP : (i - low_block + 1) * GROUP, :]
            cbuf[i] = (value + direct * dbuf[i].astype(F32)).astype(BF16)
            copy = message(cbuf.at[i], rbuf, b_send.at[i], b_recv, i)
            returns.append(copy)
            pl.when(s != i)(copy.start)
    rbuf[pl.ds(s, 1)] = cbuf[pl.ds(s, 1)]
    for j in range(BLOCKS):
        got(j, rbuf, b_send, b_recv)

    back = jnp.transpose(rbuf[...].reshape(BLOCK, BLOCK).astype(F32))
    gated[...] = (qbuf[...] * back).astype(BF16)

    sums = Links(rs_send, rs_recv)

    def project(dx, dy):
        wo_copies[dx, dy].wait()
        part[dy * 4 + dx] = dot(gated[...], wo[dy * 4 + dx])

    def half(h, dp, dq):
        return part.at[slot(h, dp, dq), pl.ds(h * 128, 128), :]

    column = (2, 1, 3, 0)

    def relay(h, e):
        snd[h, e, 0] = half(h, column[e], 2)[...].astype(BF16)
        sums.start(("Q1+", h, e), snd.at[h, e, 0, pl.ds(0, 64), :], rq.at[h, e, 0], neighbour(h, 1, 1))
        sums.start(("Q1-", h, e), snd.at[h, e, 0, pl.ds(64, 64), :], rq.at[h, e, 1], neighbour(h, 1, -1))

    for e in range(4):
        for h in (0, 1):
            if e or not h:
                project(*((column[e], 2) if h == 0 else (2, column[e])))
            relay(h, e)
    def pass_on(name, h, e, n, start, value):
        there = pl.ds(start, 64)
        snd[h, e, n, there, :] = value.astype(BF16)
        sums.start(
            (name, h, e, n), snd.at[h, e, n, there, :], rh.at[h, e, n - 1, there, :], neighbour(h, 1, 3 - 2 * n)
        )

    def free(e):
        for h in (0, 1):
            pass_on("free", h, e, 1, 64, half(h, column[e], 1)[64:128, :])
            pass_on("free", h, e, 2, 0, half(h, column[e], 3)[0:64, :])

    def joined(e):
        for h in (0, 1):
            sums.arrived(("Q1+", h, e))
            pass_on("joined", h, e, 1, 0, half(h, column[e], 1)[0:64, :] + rq[h, e, 0].astype(F32))
            sums.arrived(("Q1-", h, e))
            pass_on("joined", h, e, 2, 64, half(h, column[e], 3)[64:128, :] + rq[h, e, 1].astype(F32))

    free(0)
    for dx, dy in ((1, 1), (1, 3), (3, 1)):
        project(dx, dy)
    free(1)
    project(3, 3)
    free(2)
    for dx, dy in ((0, 1), (1, 0), (0, 3), (3, 0), (0, 0)):
        project(dx, dy)
    for e in (0, 1, 2):
        joined(e)
    free(3)
    joined(3)

    def reduced(h, e):
        for name in ("free", "joined"):
            for n in (1, 2):
                sums.arrived((name, h, e, n))
        return half(h, column[e], 0)[...] + rh[h, e, 0].astype(F32) + rh[h, e, 1].astype(F32)

    for e, sign in ((0, 2), (1, 1), (2, -1)):
        for h in (0, 1):
            psnd[h, e] = reduced(h, e).astype(BF16)
            sums.start(("P", h, e), psnd.at[h, e], rp.at[h, e], neighbour(h, 0, sign))
    for h in (0, 1):
        red[h] = reduced(h, 3)
    for h in (0, 1):
        total = red[h]
        for n in (0, 1, 2):
            sums.arrived(("P", h, n))
            total = total + rp[h, n].astype(F32)
        out[h * 128 : h * 128 + 128, :] = total.astype(BF16)

    links.finish()
    sums.finish()
    for copy in waits:
        copy.wait_send()
    for i, copy in enumerate(returns):
        pl.when(s != i)(copy.wait_send)


def per_device(tokens, in_weight, short_taps, filter_in, filter_out, rates, skip, out_weight):
    forward, inverse, feats = tables(4096)
    vmem = pl.BlockSpec(memory_space=pltpu.VMEM)
    hbm = pl.BlockSpec(memory_space=pl.ANY)
    dma = pltpu.SemaphoreType.DMA
    square = (BLOCK, BLOCK)
    scratch = [
        pltpu.VMEM((3, 3, BLOCK), F32),
        pltpu.VMEM((33, 64), F32),
        pltpu.VMEM((64, BLOCK), F32),
        pltpu.VMEM((1, BLOCK), F32),
        pltpu.VMEM((1, BLOCK), F32),
        pltpu.VMEM((16, *square), BF16),
        pltpu.VMEM((16, 3, *square), BF16),
        pltpu.VMEM((16, *square), BF16),
        pltpu.VMEM((FEAT_ROWS, 4096), F32),
        pltpu.VMEM((2, BLOCK, FREQS), BF16),
        pltpu.VMEM((2, FREQS, BLOCK), BF16),
        pltpu.VMEM((3, *square), F32),
        pltpu.VMEM((128, 128), F32),
        pltpu.VMEM((BLOCK, 64), F32),
        pltpu.VMEM((BLOCK, 128), F32),
        pltpu.VMEM((BLOCK, 128), F32),
        pltpu.VMEM(square, F32),
        pltpu.VMEM((GROUP + BLOCK, FREQS), F32),
        pltpu.VMEM((BLOCK + LAG_PAD, BLOCK), F32),
        pltpu.VMEM((BLOCK + LAG_PAD, BLOCK), F32),
        pltpu.VMEM((BLOCK + LAG_PAD, BLOCK), F32),
        pltpu.VMEM((3, EDGE, BLOCK), BF16),
        pltpu.VMEM((3, EDGE, BLOCK), BF16),
        pltpu.VMEM((3, 16 + BLOCK, BLOCK), F32),
        pltpu.VMEM(square, F32),
        pltpu.VMEM(square, F32),
        pltpu.VMEM((BLOCKS, GROUP, BLOCK), BF16),
        pltpu.VMEM((BLOCKS, GROUP, BLOCK), BF16),
        pltpu.VMEM((LAG_PAD + BLOCK, FREQS), F32),
        pltpu.VMEM((BLOCK, FREQS), F32),
        pltpu.VMEM((BLOCKS, GROUP, BLOCK), BF16),
        pltpu.VMEM((BLOCKS, GROUP, BLOCK), BF16),
        pltpu.VMEM(square, BF16),
        pltpu.VMEM((16, *square), F32),
        pltpu.VMEM((2, 4, 3, 128, BLOCK), BF16),
        pltpu.VMEM((2, 4, 2, 64, BLOCK), BF16),
        pltpu.VMEM((2, 4, 2, 128, BLOCK), BF16),
        pltpu.VMEM((2, 3, 128, BLOCK), BF16),
        pltpu.VMEM((2, 3, 128, BLOCK), BF16),
        pltpu.VMEM((2, 128, BLOCK), F32),
        pltpu.SemaphoreType.REGULAR((3,)),
        dma((9,)),
        dma((16,)),
        dma((16,)),
        dma((53,)),
        dma((53,)),
        dma((1,)),
        dma((1,)),
        dma((16,)),
        dma((16,)),
        dma((16,)),
        dma((16,)),
        dma((54,)),
        dma((54,)),
    ]
    return pl.pallas_call(
        kernel,
        out_shape=pltpu.VMEM(square, BF16),
        in_specs=[hbm] * 11,
        out_specs=vmem,
        scratch_shapes=scratch,
        compiler_params=pltpu.CompilerParams(
            collective_id=0, has_side_effects=True, vmem_limit_bytes=56 * 1024 * 1024
        ),
        name="hyena",
    )(
        tokens,
        jnp.transpose(in_weight, (1, 0, 2)),
        short_taps,
        filter_in,
        filter_out,
        rates.reshape(1, BLOCK),
        skip.reshape(1, BLOCK),
        out_weight,
        jnp.asarray(feats),
        jnp.asarray(forward),
        jnp.asarray(inverse),
    )


def solution(mesh):
    placed = (
        P("seq", "chan"),
        P(None, None, "chan"),
        P(None, None, "chan"),
        P(),
        P(None, "chan"),
        P("chan"),
        P("chan"),
        P("chan", None),
    )
    return jax.shard_map(
        per_device, mesh=mesh, in_specs=placed, out_specs=P("seq", "chan"), check_vma=False
    )
```

```python
import functools
import math

import jax
import jax.numpy as jnp
import ml_dtypes
import numpy as np
from jax import lax
from jax.experimental import pallas as pl
from jax.experimental.pallas import tpu as pltpu
from jax.sharding import PartitionSpec as P

BLOCK = 256
GROUP = 16
BLOCKS = 16
FREQS = 2 * BLOCK
FEAT_ROWS = 40
EDGE = 16
LAG_STEP = 4
LAG_PAD = (LAG_STEP - 1) * GROUP
ORDER = (8, 7, 9, 6, 10, 5, 11, 4, 12, 3, 13, 2, 14, 1, 15)
MESH_ID = pl.DeviceIdType.MESH
F32 = jnp.float32
BF16 = jnp.bfloat16


def split_two(values):
    high = values.astype(ml_dtypes.bfloat16)
    low = (values - high.astype(np.float64)).astype(ml_dtypes.bfloat16)
    return np.stack([high, low])


@functools.cache
def tables(total):
    row = np.arange(BLOCK)
    freq = np.arange(BLOCK)
    angle = 2.0 * np.pi * ((row[:, None] * freq[None, :]) % FREQS) / FREQS
    imag = -np.sin(angle)
    imag[:, 0] = 1.0 - 2.0 * (row % 2)
    forward = np.concatenate([np.cos(angle), imag], axis=1)
    angle = 2.0 * np.pi * ((freq[:, None] * (row[None, :] + BLOCK)) % FREQS) / FREQS
    real_rows = 2.0 * np.cos(angle)
    real_rows[0] = 1.0
    imag_rows = -2.0 * np.sin(angle)
    imag_rows[0] = 1.0 - 2.0 * (row % 2)
    inverse = np.concatenate([real_rows, imag_rows], axis=0) / FREQS
    place = np.arange(total)
    count = 16
    rates = 1 + np.arange(count) * (total // 4 - 1) // (count - 1)
    phase = (place[None, :] * rates[:, None]) % total
    turn = 2.0 * np.pi * phase / total
    feats = np.zeros((FEAT_ROWS, total), np.float32)
    feats[0] = place / total
    feats[1 : 1 + count] = np.cos(turn)
    feats[1 + count : 1 + 2 * count] = np.sin(turn)
    return split_two(forward), split_two(inverse), feats


def sine(x):
    turns = jnp.round(x * (1.0 / math.pi))
    r = x - turns * 3.140625
    r = r - turns * 0.0009670257568359375
    r = r - turns * 6.2771141529083252e-07
    odd = turns - 2.0 * jnp.floor(turns * 0.5)
    z = r * r
    poly = 1.0 / 6227020800.0
    for term in (-39916800.0, 362880.0, -5040.0, 120.0, -6.0):
        poly = poly * z + 1.0 / term
    value = r + r * z * poly
    return value * (1.0 - 2.0 * odd)


def dot(a, b):
    return jnp.dot(a, b, preferred_element_type=F32)


def halves(x):
    high = x.astype(BF16)
    return high, (x - high.astype(F32)).astype(BF16)


def slot(h, first, second):
    dx, dy = (first, second) if h == 0 else (second, first)
    return (dy % 4) * 4 + dx % 4


def rows(h, part):
    base = h * 128
    cut = EDGE if h else 0
    return {"f": (base, 128 - cut), "q1": (base, 64), "q2": (base + 64, 64 - cut)}[part]


class Links:
    def __init__(self, send, recv):
        self.send, self.recv, self.known = send, recv, {}

    def start(self, name, src, dst, device):
        index = len(self.known)
        copy = pltpu.make_async_remote_copy(
            src_ref=src,
            dst_ref=dst,
            send_sem=self.send.at[index],
            recv_sem=self.recv.at[index],
            device_id=device,
            device_id_type=MESH_ID,
        )
        copy.start()
        self.known[name] = copy

    def arrived(self, name):
        self.known[name].wait_recv()

    def finish(self):
        for copy in self.known.values():
            copy.wait_send()


def kernel(
    tok, win, taps_in, fin_in, fout_in, rates_in, skip_in, wout, feats, fmat, gmat,
    out,
    taps, fin, fout, rates, skip, xbuf, wbuf, wo, featbuf, fbuf, gbuf, acc, finp, fot, ratecol, skipcol, fs, aspec, sre, sim, sre2,
    edge_out, edge_in, pf, qbuf, drv, sbuf, dbuf, xs, ys, cbuf, rbuf, gated,
    part, snd, rq, rh, psnd, rp, red,
    word_sem, local_sem, w_sem, wo_sem, ag_send, ag_recv, halo_send, halo_recv, a_send, a_recv, b_send, b_recv, rs_send, rs_recv,
):
    s = lax.axis_index("seq")
    c = lax.axis_index("chan")
    x, y = lax.rem(c, 4), lax.div(c, 4)
    spots = [(dx, dy) for dy in range(4) for dx in range(4)]

    def chan_at(dx, dy):
        return lax.rem(y + dy + 4, 4) * 4 + lax.rem(x + dx + 4, 4)

    def neighbour(h, stage, sign):
        along_x = (h == 0) == (stage == 0)
        return {"chan": chan_at(sign, 0) if along_x else chan_at(0, sign)}

    z, core = lax.div(s, 2), lax.rem(s, 2)

    def plane(step):
        return {"seq": lax.rem(z + step + 8, 8) * 2 + core}

    sibling = {"seq": z * 2 + 1 - core}
    barrier = pltpu.get_barrier_semaphore()
    near = [{"chan": chan_at(step, 0)} for step in (1, -1, 2)]
    near += [{"chan": chan_at(0, step)} for step in (1, -1, 2)]
    near += [sibling, plane(1), plane(-1)]
    for device in near:
        pl.semaphore_signal(barrier, inc=1, device_id=device, device_id_type=MESH_ID)

    small = [
        pltpu.make_async_copy(src, dst, local_sem.at[4 + n])
        for n, (src, dst) in enumerate(
            ((fin_in, fin), (fout_in, fout), (rates_in, rates), (skip_in, skip), (taps_in, taps))
        )
    ]
    for copy in small:
        copy.start()
    own = pltpu.make_async_copy(tok, xbuf.at[0], local_sem.at[0])
    own.start()
    order = [(0, 0), (1, 0), (3, 0), (0, 1), (0, 3), (2, 0), (0, 2), (1, 1), (1, 3), (3, 1), (3, 3),
             (1, 2), (2, 1), (3, 2), (2, 3), (2, 2)]
    w_copies = {}
    feat_copy = pltpu.make_async_copy(feats, featbuf, local_sem.at[1])
    f_copy = pltpu.make_async_copy(fmat, fbuf, local_sem.at[2])
    g_copy = pltpu.make_async_copy(gmat, gbuf, local_sem.at[3])
    feat_copy.start()

    def start_weights(first, last):
        for n in range(first, last):
            dx, dy = order[n]
            at = pl.ds(pl.multiple_of(chan_at(-dx, -dy) * BLOCK, BLOCK), BLOCK)
            w_copies[dx, dy] = pltpu.make_async_copy(win.at[:, at, :], wbuf.at[n], w_sem.at[n])
            w_copies[dx, dy].start()

    start_weights(0, 1)
    wo_copies = {}

    pl.semaphore_wait(barrier, len(near))

    rounds = ([plane(1), plane(-1)], [plane(2), plane(-2)], [sibling])

    def tell(n):
        for device in rounds[n]:
            pl.semaphore_signal(word_sem.at[n], inc=1, device_id=device, device_id_type=MESH_ID)

    def hear(n):
        pl.semaphore_wait(word_sem.at[n], len(rounds[n]))

    links = Links(ag_send, ag_recv)

    def push(name, h, frm, to, piece, stage, sign):
        start, size = rows(h, piece)
        here = xbuf.at[slot(h, *frm), pl.ds(start, size), :]
        there = xbuf.at[slot(h, *to), pl.ds(start, size), :]
        links.start((name, h), here, there, neighbour(h, stage, sign))

    def take(*names):
        for name in names:
            for h in (0, 1):
                links.arrived((name, h))

    def multiply(blocks, first=False):
        for dx, dy in blocks:
            if (dx, dy) == (0, 0):
                w_copies[dx, dy].wait()
        for j in range(3):
            total = None if first else acc[j]
            for dx, dy in blocks:
                term = dot(xbuf[dy * 4 + dx], wbuf[order.index((dx, dy)), j])
                total = term if total is None else total + term
            acc[j] = total

    own.wait()
    tell(0)
    for h in (0, 1):
        push("P2", h, (0, 0), (2, 0), "f", 0, 2)
        push("P0+", h, (0, 0), (1, 0), "f", 0, 1)
        push("P0-", h, (0, 0), (3, 0), "f", 0, -1)
    for h in (0, 1):
        push("Q00+", h, (0, 0), (0, 1), "f", 1, 1)
        push("Q00-", h, (0, 0), (0, 3), "f", 1, -1)

    edge = pl.ds(BLOCK - EDGE, EDGE)
    for step in (1, 2, 3):
        links.start(
            ("EP", step),
            xbuf.at[0, edge, :],
            xbuf.at[step * (1 + 3 * core), edge, :],
            {"chan": chan_at(step * (1 - core), step * core)},
        )
    start_weights(1, 16)
    f_copy.start()

    for copy in small:
        copy.wait()
    finp[...] = jnp.zeros_like(finp)
    finp[0:33, 0:64] = fin[...]
    fin_t = jnp.transpose(finp[...])[0:64, 0:FEAT_ROWS]
    fot[...] = jnp.transpose(fout[...])
    ratecol[...] = jnp.transpose(jnp.broadcast_to(rates[...], (128, BLOCK)))
    skipcol[...] = jnp.transpose(jnp.broadcast_to(skip[...], (128, BLOCK)))
    mine = pl.ds(pl.multiple_of(s * GROUP, GROUP), GROUP)
    fo = fot[mine, :]
    rate = ratecol[mine, :]
    rate = jnp.concatenate([rate] * 4, axis=1)
    scale = jnp.sqrt(rate)
    feat_copy.wait()

    def filter_piece(n, carry):
        at = pl.ds(pl.multiple_of(n * 512, 512), 512)
        arg = jnp.dot(fin_t, featbuf[:, at], precision=lax.Precision.HIGHEST, preferred_element_type=F32)
        shaped = jnp.dot(fo, sine(arg), precision=lax.Precision.HIGHEST, preferred_element_type=F32)
        place = (lax.broadcasted_iota(jnp.int32, (GROUP, 512), 1) + n * 512).astype(F32)
        value = shaped * scale * jnp.exp(-rate * place)
        fs[pl.ds(pl.multiple_of(n * 32, 32), GROUP), :] = value[:, :BLOCK]
        fs[pl.ds(pl.multiple_of(n * 32 + 16, 16), GROUP), :] = value[:, BLOCK:]
        return carry

    lax.fori_loop(0, 4, filter_piece, 0)
    multiply([(0, 0)], first=True)

    take("P0+", "P0-")
    for h in (0, 1):
        for dp in (1, 3):
            push(f"Q{dp}0+", h, (dp, 0), (dp, 1), "f", 1, 1)
            push(f"Q{dp}0-", h, (dp, 0), (dp, 3), "f", 1, -1)
    take("P2")
    for h in (0, 1):
        push("Q20+", h, (2, 0), (2, 1), "f", 1, 1)
        push("Q20-", h, (2, 0), (2, 3), "f", 1, -1)
    take("Q00+", "Q00-")
    for h in (0, 1):
        push("Q01+", h, (0, 1), (0, 2), "q1", 1, 1)
        push("Q01-", h, (0, 3), (0, 2), "q2", 1, -1)
    for step in (1, 2, 3):
        links.arrived(("EP", step))
    for step in (1, 2, 3):
        for k in range(4):
            links.start(
                ("EQ", step, k),
                xbuf.at[k * (1 + 3 * core), edge, :],
                xbuf.at[k * (1 + 3 * core) + step * (4 - 3 * core), edge, :],
                {"chan": chan_at(step * core, step * (1 - core))},
            )
    hear(0)
    tell(1)
    lax.fori_loop(4, 8, filter_piece, 0)
    for dp in (1, 3):
        take(f"Q{dp}0+", f"Q{dp}0-")
        for h in (0, 1):
            push(f"Q{dp}1+", h, (dp, 1), (dp, 2), "q1", 1, 1)
            push(f"Q{dp}1-", h, (dp, 3), (dp, 2), "q2", 1, -1)

    take("Q20+", "Q20-")
    for h in (0, 1):
        push("Q21+", h, (2, 1), (2, 2), "q1", 1, 1)
        push("Q21-", h, (2, 3), (2, 2), "q2", 1, -1)

    for step in (1, 2, 3):
        for k in range(4):
            links.arrived(("EQ", step, k))
    for dx, dy in order[1:]:
        w_copies[dx, dy].wait()
    for j in range(3):
        total = None
        for dx, dy in order:
            term = dot(xbuf[dy * 4 + dx, BLOCK - EDGE :, :], wbuf[order.index((dx, dy)), j])
            total = term if total is None else total + term
        edge_out[j] = total.astype(BF16)
    halo = pltpu.make_async_remote_copy(
        src_ref=edge_out,
        dst_ref=edge_in,
        send_sem=halo_send.at[0],
        recv_sem=halo_recv.at[0],
        device_id={"seq": lax.rem(s + 1, BLOCKS)},
        device_id_type=MESH_ID,
    )
    halo.start()
    hear(1)
    tell(2)
    g_copy.start()
    for n, (dx, dy) in enumerate(spots):
        at = pl.ds(pl.multiple_of(chan_at(dx, dy) * BLOCK, BLOCK), BLOCK)
        wo_copies[dx, dy] = pltpu.make_async_copy(wout.at[:, at], wo.at[n], wo_sem.at[n])
        wo_copies[dx, dy].start()

    take("Q01+", "Q01-")
    multiply(order[1:11])
    for h, dp, block in ((0, 1, (1, 2)), (1, 1, (2, 1)), (0, 3, (3, 2)), (1, 3, (2, 3))):
        links.arrived((f"Q{dp}1+", h))
        links.arrived((f"Q{dp}1-", h))
        multiply([block])
    hear(2)
    take("Q21+", "Q21-")
    multiply([(2, 2)])

    for j in range(3):
        pf[j, 16:, :] = acc[j].astype(BF16).astype(F32)

    def short(start, size):
        branch = []
        for j in range(3):
            value = taps[0, pl.ds(j, 1), :] * pf[j, pl.ds(16 + start, size), :]
            value = value + taps[1, pl.ds(j, 1), :] * pf[j, pl.ds(15 + start, size), :]
            branch.append(value + taps[2, pl.ds(j, 1), :] * pf[j, pl.ds(14 + start, size), :])
        qbuf[pl.ds(start, size), :] = branch[0]
        drv[pl.ds(start, size), :] = branch[1] * branch[2]

    halo.wait_recv()
    live = (s > 0).astype(F32)
    for j in range(3):
        pf[j, 0:16, :] = edge_in[j].astype(F32) * live
    for start in range(0, BLOCK, 32):
        short(start, 32)

    sbuf[...] = jnp.transpose(drv[...]).astype(BF16).reshape(BLOCKS, GROUP, BLOCK)

    def message(src, dst, send, recv, other):
        return pltpu.make_async_remote_copy(
            src_ref=src,
            dst_ref=dst.at[s],
            send_sem=send,
            recv_sem=recv.at[s],
            device_id={"seq": other},
            device_id_type=MESH_ID,
        )

    def got(j, buffer, send, recv):
        @pl.when(s != j)
        def _():
            pltpu.make_async_remote_copy(
                src_ref=buffer.at[j],
                dst_ref=buffer.at[j],
                send_sem=send.at[0],
                recv_sem=recv.at[j],
                device_id={"seq": lax.rem(s + 1, BLOCKS)},
                device_id_type=MESH_ID,
            ).wait_recv()

    waits = [halo]
    for k in ORDER:
        other = lax.rem(s + k, BLOCKS)
        copy = message(sbuf.at[other], dbuf, a_send.at[k], a_recv, other)
        copy.start()
        waits.append(copy)
    dbuf[pl.ds(s, 1)] = sbuf[pl.ds(s, 1)]
    f_copy.wait()
    high, low = halves(fs[...])
    aspec[0:GROUP, :] = jnp.zeros((GROUP, FREQS), F32)
    aspec[GROUP:, :] = dot(high, fbuf[0]) + dot(low, fbuf[0]) + dot(high, fbuf[1])
    lane = lax.broadcasted_iota(jnp.int32, (GROUP, BLOCK), 1)
    parity = 1.0 - 2.0 * lax.rem(lane, 2).astype(F32)

    for table in (sre, sim, sre2):
        table[BLOCK:, :] = jnp.zeros((LAG_PAD, BLOCK), F32)

    def lag_piece(n, carry):
        before = pl.ds(pl.multiple_of(n * GROUP, GROUP), GROUP)
        after = pl.ds(pl.multiple_of(n * GROUP + GROUP, GROUP), GROUP)
        re = aspec[before, 0:BLOCK] + parity * aspec[after, 0:BLOCK]
        im = aspec[before, BLOCK:] + parity * aspec[after, BLOCK:]
        sre[before, :] = re
        sim[before, :] = jnp.where(lane == 0, 0.0, im)
        sre2[before, :] = jnp.where(lane == 0, im, re)
        return carry

    lax.fori_loop(0, BLOCKS, lag_piece, 0)

    xs[0:LAG_PAD, :] = jnp.zeros((LAG_PAD, FREQS), F32)
    direct = skipcol[mine, :]
    direct = jnp.concatenate([direct, direct], axis=1)
    g_copy.wait()

    def spectrum(i):
        def lags(turn, total):
            re, im = total
            for d in range(LAG_STEP):
                d = turn * LAG_STEP + d
                at = pl.ds(pl.multiple_of((i - d) * GROUP + LAG_PAD, GROUP), GROUP)
                by = pl.ds(pl.multiple_of(d * GROUP, GROUP), GROUP)
                xr, xi = xs[at, 0:BLOCK], xs[at, BLOCK:]
                part_im = sim[by, :]
                re = re + (xr * sre[by, :] - xi * part_im)
                im = im + (xr * part_im + xi * sre2[by, :])
            return re, im

        zero = jnp.zeros((GROUP, BLOCK), F32)
        re, im = lax.fori_loop(0, (i + LAG_STEP) // LAG_STEP, lags, (zero, zero))
        ys[i * GROUP : (i + 1) * GROUP, 0:BLOCK] = re
        ys[i * GROUP : (i + 1) * GROUP, BLOCK:] = im

    returns = []
    for low_block, high_block in ((0, 4), (4, 8), (8, 16)):
        count = (high_block - low_block) * GROUP
        for j in range(low_block, high_block):
            got(j, dbuf, a_send, a_recv)
        some = slice(low_block * GROUP, high_block * GROUP)
        drive = dbuf[low_block:high_block].reshape(count, BLOCK)
        xs[LAG_PAD + some.start : LAG_PAD + some.stop, :] = dot(drive, fbuf[0]) + dot(drive, fbuf[1])
        for i in range(low_block, high_block):
            spectrum(i)
        high, low = halves(ys[some, :])
        both = dot(jnp.concatenate([high, low], axis=0), gbuf[0])
        conv = both[:count] + both[count:] + dot(high, gbuf[1])
        for i in range(low_block, high_block):
            value = conv[(i - low_block) * GROUP : (i - low_block + 1) * GROUP, :]
            cbuf[i] = (value + direct * dbuf[i].astype(F32)).astype(BF16)
            copy = message(cbuf.at[i], rbuf, b_send.at[i], b_recv, i)
            returns.append(copy)
            pl.when(s != i)(copy.start)
    rbuf[pl.ds(s, 1)] = cbuf[pl.ds(s, 1)]
    for j in range(BLOCKS):
        got(j, rbuf, b_send, b_recv)

    back = jnp.transpose(rbuf[...].reshape(BLOCK, BLOCK).astype(F32))
    gated[...] = (qbuf[...] * back).astype(BF16)

    sums = Links(rs_send, rs_recv)

    def project(dx, dy):
        wo_copies[dx, dy].wait()
        part[dy * 4 + dx] = dot(gated[...], wo[dy * 4 + dx])

    def half(h, dp, dq):
        return part.at[slot(h, dp, dq), pl.ds(h * 128, 128), :]

    column = (2, 1, 3, 0)

    def relay(h, e):
        snd[h, e, 0] = half(h, column[e], 2)[...].astype(BF16)
        sums.start(("Q1+", h, e), snd.at[h, e, 0, pl.ds(0, 64), :], rq.at[h, e, 0], neighbour(h, 1, 1))
        sums.start(("Q1-", h, e), snd.at[h, e, 0, pl.ds(64, 64), :], rq.at[h, e, 1], neighbour(h, 1, -1))

    for e in range(4):
        for h in (0, 1):
            if e or not h:
                project(*((column[e], 2) if h == 0 else (2, column[e])))
            relay(h, e)
    def pass_on(name, h, e, n, start, value):
        there = pl.ds(start, 64)
        snd[h, e, n, there, :] = value.astype(BF16)
        sums.start(
            (name, h, e, n), snd.at[h, e, n, there, :], rh.at[h, e, n - 1, there, :], neighbour(h, 1, 3 - 2 * n)
        )

    def free(e):
        for h in (0, 1):
            pass_on("free", h, e, 1, 64, half(h, column[e], 1)[64:128, :])
            pass_on("free", h, e, 2, 0, half(h, column[e], 3)[0:64, :])

    def joined(e):
        for h in (0, 1):
            sums.arrived(("Q1+", h, e))
            pass_on("joined", h, e, 1, 0, half(h, column[e], 1)[0:64, :] + rq[h, e, 0].astype(F32))
            sums.arrived(("Q1-", h, e))
            pass_on("joined", h, e, 2, 64, half(h, column[e], 3)[64:128, :] + rq[h, e, 1].astype(F32))

    free(0)
    for dx, dy in ((1, 1), (1, 3), (3, 1)):
        project(dx, dy)
    free(1)
    project(3, 3)
    free(2)
    for dx, dy in ((0, 1), (1, 0), (0, 3), (3, 0), (0, 0)):
        project(dx, dy)
    for e in (0, 1, 2):
        joined(e)
    free(3)
    joined(3)

    def reduced(h, e):
        for name in ("free", "joined"):
            for n in (1, 2):
                sums.arrived((name, h, e, n))
        return half(h, column[e], 0)[...] + rh[h, e, 0].astype(F32) + rh[h, e, 1].astype(F32)

    for e, sign in ((0, 2), (1, 1), (2, -1)):
        for h in (0, 1):
            psnd[h, e] = reduced(h, e).astype(BF16)
            sums.start(("P", h, e), psnd.at[h, e], rp.at[h, e], neighbour(h, 0, sign))
    for h in (0, 1):
        red[h] = reduced(h, 3)
    for h in (0, 1):
        total = red[h]
        for n in (0, 1, 2):
            sums.arrived(("P", h, n))
            total = total + rp[h, n].astype(F32)
        out[h * 128 : h * 128 + 128, :] = total.astype(BF16)

    links.finish()
    sums.finish()
    for copy in waits:
        copy.wait_send()
    for i, copy in enumerate(returns):
        pl.when(s != i)(copy.wait_send)


def per_device(tokens, in_weight, short_taps, filter_in, filter_out, rates, skip, out_weight):
    forward, inverse, feats = tables(4096)
    vmem = pl.BlockSpec(memory_space=pltpu.VMEM)
    hbm = pl.BlockSpec(memory_space=pl.ANY)
    dma = pltpu.SemaphoreType.DMA
    square = (BLOCK, BLOCK)
    scratch = [
        pltpu.VMEM((3, 3, BLOCK), F32),
        pltpu.VMEM((33, 64), F32),
        pltpu.VMEM((64, BLOCK), F32),
        pltpu.VMEM((1, BLOCK), F32),
        pltpu.VMEM((1, BLOCK), F32),
        pltpu.VMEM((16, *square), BF16),
        pltpu.VMEM((16, 3, *square), BF16),
        pltpu.VMEM((16, *square), BF16),
        pltpu.VMEM((FEAT_ROWS, 4096), F32),
        pltpu.VMEM((2, BLOCK, FREQS), BF16),
        pltpu.VMEM((2, FREQS, BLOCK), BF16),
        pltpu.VMEM((3, *square), F32),
        pltpu.VMEM((128, 128), F32),
        pltpu.VMEM((BLOCK, 64), F32),
        pltpu.VMEM((BLOCK, 128), F32),
        pltpu.VMEM((BLOCK, 128), F32),
        pltpu.VMEM(square, F32),
        pltpu.VMEM((GROUP + BLOCK, FREQS), F32),
        pltpu.VMEM((BLOCK + LAG_PAD, BLOCK), F32),
        pltpu.VMEM((BLOCK + LAG_PAD, BLOCK), F32),
        pltpu.VMEM((BLOCK + LAG_PAD, BLOCK), F32),
        pltpu.VMEM((3, EDGE, BLOCK), BF16),
        pltpu.VMEM((3, EDGE, BLOCK), BF16),
        pltpu.VMEM((3, 16 + BLOCK, BLOCK), F32),
        pltpu.VMEM(square, F32),
        pltpu.VMEM(square, F32),
        pltpu.VMEM((BLOCKS, GROUP, BLOCK), BF16),
        pltpu.VMEM((BLOCKS, GROUP, BLOCK), BF16),
        pltpu.VMEM((LAG_PAD + BLOCK, FREQS), F32),
        pltpu.VMEM((BLOCK, FREQS), F32),
        pltpu.VMEM((BLOCKS, GROUP, BLOCK), BF16),
        pltpu.VMEM((BLOCKS, GROUP, BLOCK), BF16),
        pltpu.VMEM(square, BF16),
        pltpu.VMEM((16, *square), F32),
        pltpu.VMEM((2, 4, 3, 128, BLOCK), BF16),
        pltpu.VMEM((2, 4, 2, 64, BLOCK), BF16),
        pltpu.VMEM((2, 4, 2, 128, BLOCK), BF16),
        pltpu.VMEM((2, 3, 128, BLOCK), BF16),
        pltpu.VMEM((2, 3, 128, BLOCK), BF16),
        pltpu.VMEM((2, 128, BLOCK), F32),
        pltpu.SemaphoreType.REGULAR((3,)),
        dma((9,)),
        dma((16,)),
        dma((16,)),
        dma((53,)),
        dma((53,)),
        dma((1,)),
        dma((1,)),
        dma((16,)),
        dma((16,)),
        dma((16,)),
        dma((16,)),
        dma((54,)),
        dma((54,)),
    ]
    return pl.pallas_call(
        kernel,
        out_shape=pltpu.VMEM(square, BF16),
        in_specs=[hbm] * 11,
        out_specs=vmem,
        scratch_shapes=scratch,
        compiler_params=pltpu.CompilerParams(
            collective_id=0, has_side_effects=True, vmem_limit_bytes=56 * 1024 * 1024
        ),
        name="hyena",
    )(
        tokens,
        jnp.transpose(in_weight, (1, 0, 2)),
        short_taps,
        filter_in,
        filter_out,
        rates.reshape(1, BLOCK),
        skip.reshape(1, BLOCK),
        out_weight,
        jnp.asarray(feats),
        jnp.asarray(forward),
        jnp.asarray(inverse),
    )


def solution(mesh):
    placed = (
        P("seq", "chan"),
        P(None, None, "chan"),
        P(None, None, "chan"),
        P(),
        P(None, "chan"),
        P("chan"),
        P("chan"),
        P("chan", None),
    )
    return jax.shard_map(
        per_device, mesh=mesh, in_specs=placed, out_specs=P("seq", "chan"), check_vma=False
    )
```

```python
import functools
import math

import jax
import jax.numpy as jnp
import ml_dtypes
import numpy as np
from jax import lax
from jax.experimental import pallas as pl
from jax.experimental.pallas import tpu as pltpu
from jax.sharding import PartitionSpec as P

BLOCK = 256
GROUP = 16
BLOCKS = 16
FREQS = 2 * BLOCK
FEAT_ROWS = 40
EDGE = 16
LAG_STEP = 4
LAG_PAD = (LAG_STEP - 1) * GROUP
ORDER = (8, 7, 9, 6, 10, 5, 11, 4, 12, 3, 13, 2, 14, 1, 15)
MESH_ID = pl.DeviceIdType.MESH
F32 = jnp.float32
BF16 = jnp.bfloat16


def split_two(values):
    high = values.astype(ml_dtypes.bfloat16)
    low = (values - high.astype(np.float64)).astype(ml_dtypes.bfloat16)
    return np.stack([high, low])


@functools.cache
def tables(total):
    row = np.arange(BLOCK)
    freq = np.arange(BLOCK)
    angle = 2.0 * np.pi * ((row[:, None] * freq[None, :]) % FREQS) / FREQS
    imag = -np.sin(angle)
    imag[:, 0] = 1.0 - 2.0 * (row % 2)
    forward = np.concatenate([np.cos(angle), imag], axis=1)
    angle = 2.0 * np.pi * ((freq[:, None] * (row[None, :] + BLOCK)) % FREQS) / FREQS
    real_rows = 2.0 * np.cos(angle)
    real_rows[0] = 1.0
    imag_rows = -2.0 * np.sin(angle)
    imag_rows[0] = 1.0 - 2.0 * (row % 2)
    inverse = np.concatenate([real_rows, imag_rows], axis=0) / FREQS
    place = np.arange(total)
    count = 16
    rates = 1 + np.arange(count) * (total // 4 - 1) // (count - 1)
    phase = (place[None, :] * rates[:, None]) % total
    turn = 2.0 * np.pi * phase / total
    feats = np.zeros((FEAT_ROWS, total), np.float32)
    feats[0] = place / total
    feats[1 : 1 + count] = np.cos(turn)
    feats[1 + count : 1 + 2 * count] = np.sin(turn)
    return split_two(forward), split_two(inverse), feats


def sine(x):
    turns = jnp.round(x * (1.0 / math.pi))
    r = x - turns * 3.140625
    r = r - turns * 0.0009670257568359375
    r = r - turns * 6.2771141529083252e-07
    odd = turns - 2.0 * jnp.floor(turns * 0.5)
    z = r * r
    poly = 1.0 / 6227020800.0
    for term in (-39916800.0, 362880.0, -5040.0, 120.0, -6.0):
        poly = poly * z + 1.0 / term
    value = r + r * z * poly
    return value * (1.0 - 2.0 * odd)


def dot(a, b):
    return jnp.dot(a, b, preferred_element_type=F32)


def halves(x):
    high = x.astype(BF16)
    return high, (x - high.astype(F32)).astype(BF16)


def slot(h, first, second):
    dx, dy = (first, second) if h == 0 else (second, first)
    return (dy % 4) * 4 + dx % 4


def rows(h, part):
    base = h * 128
    cut = EDGE if h else 0
    return {"f": (base, 128 - cut), "q1": (base, 64), "q2": (base + 64, 64 - cut)}[part]


class Links:
    def __init__(self, send, recv):
        self.send, self.recv, self.known = send, recv, {}

    def start(self, name, src, dst, device):
        index = len(self.known)
        copy = pltpu.make_async_remote_copy(
            src_ref=src,
            dst_ref=dst,
            send_sem=self.send.at[index],
            recv_sem=self.recv.at[index],
            device_id=device,
            device_id_type=MESH_ID,
        )
        copy.start()
        self.known[name] = copy

    def arrived(self, name):
        self.known[name].wait_recv()

    def finish(self):
        for copy in self.known.values():
            copy.wait_send()


def kernel(
    tok, win, taps_in, fin_in, fout_in, rates_in, skip_in, wout, feats, fmat, gmat,
    out,
    taps, fin, fout, rates, skip, xbuf, wbuf, wo, featbuf, fbuf, gbuf, acc, finp, fot, ratecol, skipcol, fs, aspec, sre, sim, sre2,
    edge_out, edge_in, pf, qbuf, drv, sbuf, dbuf, xs, ys, cbuf, rbuf, gated,
    part, snd, rq, rh, psnd, rp, red,
    word_sem, local_sem, w_sem, wo_sem, ag_send, ag_recv, halo_send, halo_recv, a_send, a_recv, b_send, b_recv, rs_send, rs_recv,
):
    s = lax.axis_index("seq")
    c = lax.axis_index("chan")
    x, y = lax.rem(c, 4), lax.div(c, 4)
    spots = [(dx, dy) for dy in range(4) for dx in range(4)]

    def chan_at(dx, dy):
        return lax.rem(y + dy + 4, 4) * 4 + lax.rem(x + dx + 4, 4)

    def neighbour(h, stage, sign):
        along_x = (h == 0) == (stage == 0)
        return {"chan": chan_at(sign, 0) if along_x else chan_at(0, sign)}

    z, core = lax.div(s, 2), lax.rem(s, 2)

    def plane(step):
        return {"seq": lax.rem(z + step + 8, 8) * 2 + core}

    sibling = {"seq": z * 2 + 1 - core}
    barrier = pltpu.get_barrier_semaphore()
    near = [{"chan": chan_at(step, 0)} for step in (1, -1, 2)]
    near += [{"chan": chan_at(0, step)} for step in (1, -1, 2)]
    near += [sibling]
    for device in near:
        pl.semaphore_signal(barrier, inc=1, device_id=device, device_id_type=MESH_ID)

    def planes(step):
        return (z < 8 - step).astype(jnp.int32) + (z >= step).astype(jnp.int32)

    def greet(semaphore, step):
        for there, sign in ((z < 8 - step, step), (z >= step, -step)):

            @pl.when(there)
            def _():
                pl.semaphore_signal(semaphore, inc=1, device_id=plane(sign), device_id_type=MESH_ID)

    greet(barrier, 1)

    small = [
        pltpu.make_async_copy(src, dst, local_sem.at[4 + n])
        for n, (src, dst) in enumerate(
            ((fin_in, fin), (fout_in, fout), (rates_in, rates), (skip_in, skip), (taps_in, taps))
        )
    ]
    for copy in small:
        copy.start()
    own = pltpu.make_async_copy(tok, xbuf.at[0], local_sem.at[0])
    own.start()
    order = [(0, 0), (1, 0), (3, 0), (0, 1), (0, 3), (2, 0), (0, 2), (1, 1), (1, 3), (3, 1), (3, 3),
             (1, 2), (2, 1), (3, 2), (2, 3), (2, 2)]
    w_copies = {}
    feat_copy = pltpu.make_async_copy(feats, featbuf, local_sem.at[1])
    f_copy = pltpu.make_async_copy(fmat, fbuf, local_sem.at[2])
    g_copy = pltpu.make_async_copy(gmat, gbuf, local_sem.at[3])
    feat_copy.start()

    def start_weights(first, last):
        for n in range(first, last):
            dx, dy = order[n]
            at = pl.ds(pl.multiple_of(chan_at(-dx, -dy) * BLOCK, BLOCK), BLOCK)
            w_copies[dx, dy] = pltpu.make_async_copy(win.at[:, at, :], wbuf.at[n], w_sem.at[n])
            w_copies[dx, dy].start()

    start_weights(0, 1)
    wo_copies = {}

    pl.semaphore_wait(barrier, len(near) + planes(1))

    def tell(n):
        if n == 3:
            pl.semaphore_signal(word_sem.at[n], inc=1, device_id=sibling, device_id_type=MESH_ID)
        else:
            greet(word_sem.at[n], 1 << n)

    def hear(n):
        pl.semaphore_wait(word_sem.at[n], 1 if n == 3 else planes(1 << n))

    links = Links(ag_send, ag_recv)

    def push(name, h, frm, to, piece, stage, sign):
        start, size = rows(h, piece)
        here = xbuf.at[slot(h, *frm), pl.ds(start, size), :]
        there = xbuf.at[slot(h, *to), pl.ds(start, size), :]
        links.start((name, h), here, there, neighbour(h, stage, sign))

    def take(*names):
        for name in names:
            for h in (0, 1):
                links.arrived((name, h))

    def multiply(blocks, first=False):
        for dx, dy in blocks:
            if (dx, dy) == (0, 0):
                w_copies[dx, dy].wait()
        for j in range(3):
            total = None if first else acc[j]
            for dx, dy in blocks:
                term = dot(xbuf[dy * 4 + dx], wbuf[order.index((dx, dy)), j])
                total = term if total is None else total + term
            acc[j] = total

    own.wait()
    tell(0)
    for h in (0, 1):
        push("P2", h, (0, 0), (2, 0), "f", 0, 2)
        push("P0+", h, (0, 0), (1, 0), "f", 0, 1)
        push("P0-", h, (0, 0), (3, 0), "f", 0, -1)
    for h in (0, 1):
        push("Q00+", h, (0, 0), (0, 1), "f", 1, 1)
        push("Q00-", h, (0, 0), (0, 3), "f", 1, -1)

    edge = pl.ds(BLOCK - EDGE, EDGE)
    for step in (1, 2, 3):
        links.start(
            ("EP", step),
            xbuf.at[0, edge, :],
            xbuf.at[step * (1 + 3 * core), edge, :],
            {"chan": chan_at(step * (1 - core), step * core)},
        )
    start_weights(1, 16)
    f_copy.start()

    for copy in small:
        copy.wait()
    finp[...] = jnp.zeros_like(finp)
    finp[0:33, 0:64] = fin[...]
    fin_t = jnp.transpose(finp[...])[0:64, 0:FEAT_ROWS]
    fot[...] = jnp.transpose(fout[...])
    ratecol[...] = jnp.transpose(jnp.broadcast_to(rates[...], (128, BLOCK)))
    skipcol[...] = jnp.transpose(jnp.broadcast_to(skip[...], (128, BLOCK)))
    mine = pl.ds(pl.multiple_of(s * GROUP, GROUP), GROUP)
    fo = fot[mine, :]
    rate = ratecol[mine, :]
    rate = jnp.concatenate([rate] * 4, axis=1)
    scale = jnp.sqrt(rate)
    feat_copy.wait()

    def filter_piece(n, carry):
        at = pl.ds(pl.multiple_of(n * 512, 512), 512)
        arg = jnp.dot(fin_t, featbuf[:, at], precision=lax.Precision.HIGHEST, preferred_element_type=F32)
        shaped = jnp.dot(fo, sine(arg), precision=lax.Precision.HIGHEST, preferred_element_type=F32)
        place = (lax.broadcasted_iota(jnp.int32, (GROUP, 512), 1) + n * 512).astype(F32)
        value = shaped * scale * jnp.exp(-rate * place)
        fs[pl.ds(pl.multiple_of(n * 32, 32), GROUP), :] = value[:, :BLOCK]
        fs[pl.ds(pl.multiple_of(n * 32 + 16, 16), GROUP), :] = value[:, BLOCK:]
        return carry

    lax.fori_loop(0, 4, filter_piece, 0)
    multiply([(0, 0)], first=True)

    take("P0+", "P0-")
    for h in (0, 1):
        for dp in (1, 3):
            push(f"Q{dp}0+", h, (dp, 0), (dp, 1), "f", 1, 1)
            push(f"Q{dp}0-", h, (dp, 0), (dp, 3), "f", 1, -1)
    take("P2")
    for h in (0, 1):
        push("Q20+", h, (2, 0), (2, 1), "f", 1, 1)
        push("Q20-", h, (2, 0), (2, 3), "f", 1, -1)
    take("Q00+", "Q00-")
    for h in (0, 1):
        push("Q01+", h, (0, 1), (0, 2), "q1", 1, 1)
        push("Q01-", h, (0, 3), (0, 2), "q2", 1, -1)
    for step in (1, 2, 3):
        links.arrived(("EP", step))
    for step in (1, 2, 3):
        for k in range(4):
            links.start(
                ("EQ", step, k),
                xbuf.at[k * (1 + 3 * core), edge, :],
                xbuf.at[k * (1 + 3 * core) + step * (4 - 3 * core), edge, :],
                {"chan": chan_at(step * core, step * (1 - core))},
            )
    hear(0)
    tell(1)
    lax.fori_loop(4, 8, filter_piece, 0)
    for dp in (1, 3):
        take(f"Q{dp}0+", f"Q{dp}0-")
        for h in (0, 1):
            push(f"Q{dp}1+", h, (dp, 1), (dp, 2), "q1", 1, 1)
            push(f"Q{dp}1-", h, (dp, 3), (dp, 2), "q2", 1, -1)

    take("Q20+", "Q20-")
    for h in (0, 1):
        push("Q21+", h, (2, 1), (2, 2), "q1", 1, 1)
        push("Q21-", h, (2, 3), (2, 2), "q2", 1, -1)

    hear(1)
    tell(2)

    for step in (1, 2, 3):
        for k in range(4):
            links.arrived(("EQ", step, k))
    for dx, dy in order[1:]:
        w_copies[dx, dy].wait()
    for j in range(3):
        total = None
        for dx, dy in order:
            term = dot(xbuf[dy * 4 + dx, BLOCK - EDGE :, :], wbuf[order.index((dx, dy)), j])
            total = term if total is None else total + term
        edge_out[j] = total.astype(BF16)
    halo = pltpu.make_async_remote_copy(
        src_ref=edge_out,
        dst_ref=edge_in,
        send_sem=halo_send.at[0],
        recv_sem=halo_recv.at[0],
        device_id={"seq": lax.rem(s + 1, BLOCKS)},
        device_id_type=MESH_ID,
    )
    pl.when(s < BLOCKS - 1)(halo.start)
    g_copy.start()
    for n, (dx, dy) in enumerate(spots):
        at = pl.ds(pl.multiple_of(chan_at(dx, dy) * BLOCK, BLOCK), BLOCK)
        wo_copies[dx, dy] = pltpu.make_async_copy(wout.at[:, at], wo.at[n], wo_sem.at[n])
        wo_copies[dx, dy].start()

    take("Q01+", "Q01-")
    multiply(order[1:11])
    hear(2)
    tell(3)
    for h, dp, block in ((0, 1, (1, 2)), (1, 1, (2, 1)), (0, 3, (3, 2)), (1, 3, (2, 3))):
        links.arrived((f"Q{dp}1+", h))
        links.arrived((f"Q{dp}1-", h))
        multiply([block])
    take("Q21+", "Q21-")
    multiply([(2, 2)])

    for j in range(3):
        pf[j, 16:, :] = acc[j].astype(BF16).astype(F32)

    def short(start, size):
        branch = []
        for j in range(3):
            value = taps[0, pl.ds(j, 1), :] * pf[j, pl.ds(16 + start, size), :]
            value = value + taps[1, pl.ds(j, 1), :] * pf[j, pl.ds(15 + start, size), :]
            branch.append(value + taps[2, pl.ds(j, 1), :] * pf[j, pl.ds(14 + start, size), :])
        qbuf[pl.ds(start, size), :] = branch[0]
        drv[pl.ds(start, size), :] = branch[1] * branch[2]

    pl.when(s > 0)(halo.wait_recv)

    @pl.when(s == 0)
    def _():
        edge_in[...] = jnp.zeros_like(edge_in)

    for j in range(3):
        pf[j, 0:16, :] = edge_in[j].astype(F32)
    for start in range(0, BLOCK, 32):
        short(start, 32)

    sbuf[...] = jnp.transpose(drv[...]).astype(BF16).reshape(BLOCKS, GROUP, BLOCK)

    def message(src, dst, send, recv, other):
        return pltpu.make_async_remote_copy(
            src_ref=src,
            dst_ref=dst.at[s],
            send_sem=send,
            recv_sem=recv.at[s],
            device_id={"seq": other},
            device_id_type=MESH_ID,
        )

    def got(j, buffer, send, recv):
        @pl.when(s != j)
        def _():
            pltpu.make_async_remote_copy(
                src_ref=buffer.at[j],
                dst_ref=buffer.at[j],
                send_sem=send.at[0],
                recv_sem=recv.at[j],
                device_id={"seq": lax.rem(s + 1, BLOCKS)},
                device_id_type=MESH_ID,
            ).wait_recv()

    hear(3)
    waits = []
    for k in ORDER:
        other = lax.rem(s + k, BLOCKS)
        copy = message(sbuf.at[other], dbuf, a_send.at[k], a_recv, other)
        copy.start()
        waits.append(copy)
    dbuf[pl.ds(s, 1)] = sbuf[pl.ds(s, 1)]
    f_copy.wait()
    aspec[0:GROUP, :] = jnp.zeros((GROUP, FREQS), F32)
    lane = lax.broadcasted_iota(jnp.int32, (GROUP, BLOCK), 1)
    parity = 1.0 - 2.0 * lax.rem(lane, 2).astype(F32)

    for table in (sre, sim, sre2):
        table[BLOCK:, :] = jnp.zeros((LAG_PAD, BLOCK), F32)

    def lag_piece(n, carry):
        before = pl.ds(pl.multiple_of(n * GROUP, GROUP), GROUP)
        after = pl.ds(pl.multiple_of(n * GROUP + GROUP, GROUP), GROUP)
        re = aspec[before, 0:BLOCK] + parity * aspec[after, 0:BLOCK]
        im = aspec[before, BLOCK:] + parity * aspec[after, BLOCK:]
        sre[before, :] = re
        sim[before, :] = jnp.where(lane == 0, 0.0, im)
        sre2[before, :] = jnp.where(lane == 0, im, re)
        return carry

    def lag_spectra(first, last):
        high, low = halves(fs[first * GROUP : last * GROUP, :])
        spectra = dot(high, fbuf[0]) + dot(low, fbuf[0]) + dot(high, fbuf[1])
        aspec[(first + 1) * GROUP : (last + 1) * GROUP, :] = spectra
        lax.fori_loop(first, last, lag_piece, 0)

    lag_spectra(0, 4)

    xs[0:LAG_PAD, :] = jnp.zeros((LAG_PAD, FREQS), F32)
    direct = skipcol[mine, :]
    direct = jnp.concatenate([direct, direct], axis=1)
    g_copy.wait()

    def spectrum(i):
        def lags(turn, total):
            re, im = total
            for d in range(LAG_STEP):
                d = turn * LAG_STEP + d
                at = pl.ds(pl.multiple_of((i - d) * GROUP + LAG_PAD, GROUP), GROUP)
                by = pl.ds(pl.multiple_of(d * GROUP, GROUP), GROUP)
                xr, xi = xs[at, 0:BLOCK], xs[at, BLOCK:]
                part_im = sim[by, :]
                re = re + (xr * sre[by, :] - xi * part_im)
                im = im + (xr * part_im + xi * sre2[by, :])
            return re, im

        zero = jnp.zeros((GROUP, BLOCK), F32)
        re, im = lax.fori_loop(0, (i + LAG_STEP) // LAG_STEP, lags, (zero, zero))
        ys[i * GROUP : (i + 1) * GROUP, 0:BLOCK] = re
        ys[i * GROUP : (i + 1) * GROUP, BLOCK:] = im

    returns = []
    for low_block, high_block in ((0, 4), (4, 8), (8, 16)):
        count = (high_block - low_block) * GROUP
        for j in range(low_block, high_block):
            got(j, dbuf, a_send, a_recv)
        some = slice(low_block * GROUP, high_block * GROUP)
        drive = dbuf[low_block:high_block].reshape(count, BLOCK)
        xs[LAG_PAD + some.start : LAG_PAD + some.stop, :] = dot(drive, fbuf[0]) + dot(drive, fbuf[1])
        for i in range(low_block, high_block):
            spectrum(i)
        high, low = halves(ys[some, :])
        both = dot(jnp.concatenate([high, low], axis=0), gbuf[0])
        conv = both[:count] + both[count:] + dot(high, gbuf[1])
        for i in range(low_block, high_block):
            value = conv[(i - low_block) * GROUP : (i - low_block + 1) * GROUP, :]
            cbuf[i] = (value + direct * dbuf[i].astype(F32)).astype(BF16)
            copy = message(cbuf.at[i], rbuf, b_send.at[i], b_recv, i)
            returns.append(copy)
            pl.when(s != i)(copy.start)
        if low_block == 0:
            lag_spectra(4, BLOCKS)
    rbuf[pl.ds(s, 1)] = cbuf[pl.ds(s, 1)]
    for j in range(BLOCKS):
        got(j, rbuf, b_send, b_recv)

    back = jnp.transpose(rbuf[...].reshape(BLOCK, BLOCK).astype(F32))
    gated[...] = (qbuf[...] * back).astype(BF16)

    sums = Links(rs_send, rs_recv)

    def project(dx, dy):
        wo_copies[dx, dy].wait()
        part[dy * 4 + dx] = dot(gated[...], wo[dy * 4 + dx])

    def half(h, dp, dq):
        return part.at[slot(h, dp, dq), pl.ds(h * 128, 128), :]

    column = (2, 1, 3, 0)

    def relay(h, e):
        snd[h, e, 0] = half(h, column[e], 2)[...].astype(BF16)
        sums.start(("Q1+", h, e), snd.at[h, e, 0, pl.ds(0, 64), :], rq.at[h, e, 0], neighbour(h, 1, 1))
        sums.start(("Q1-", h, e), snd.at[h, e, 0, pl.ds(64, 64), :], rq.at[h, e, 1], neighbour(h, 1, -1))

    for e in range(4):
        for h in (0, 1):
            if e or not h:
                project(*((column[e], 2) if h == 0 else (2, column[e])))
            relay(h, e)
    def pass_on(name, h, e, n, start, value):
        there = pl.ds(start, 64)
        snd[h, e, n, there, :] = value.astype(BF16)
        sums.start(
            (name, h, e, n), snd.at[h, e, n, there, :], rh.at[h, e, n - 1, there, :], neighbour(h, 1, 3 - 2 * n)
        )

    def free(e):
        for h in (0, 1):
            pass_on("free", h, e, 1, 64, half(h, column[e], 1)[64:128, :])
            pass_on("free", h, e, 2, 0, half(h, column[e], 3)[0:64, :])

    def joined(e):
        for h in (0, 1):
            sums.arrived(("Q1+", h, e))
            pass_on("joined", h, e, 1, 0, half(h, column[e], 1)[0:64, :] + rq[h, e, 0].astype(F32))
            sums.arrived(("Q1-", h, e))
            pass_on("joined", h, e, 2, 64, half(h, column[e], 3)[64:128, :] + rq[h, e, 1].astype(F32))

    free(0)
    for dx, dy in ((1, 1), (1, 3), (3, 1)):
        project(dx, dy)
    free(1)
    project(3, 3)
    free(2)
    for dx, dy in ((0, 1), (1, 0), (0, 3), (3, 0), (0, 0)):
        project(dx, dy)
    for e in (0, 1, 2):
        joined(e)
    free(3)
    joined(3)

    def reduced(h, e):
        for name in ("free", "joined"):
            for n in (1, 2):
                sums.arrived((name, h, e, n))
        return half(h, column[e], 0)[...] + rh[h, e, 0].astype(F32) + rh[h, e, 1].astype(F32)

    for e, sign in ((0, 2), (1, 1), (2, -1)):
        for h in (0, 1):
            psnd[h, e] = reduced(h, e).astype(BF16)
            sums.start(("P", h, e), psnd.at[h, e], rp.at[h, e], neighbour(h, 0, sign))
    for h in (0, 1):
        red[h] = reduced(h, 3)
    for h in (0, 1):
        total = red[h]
        for n in (0, 1, 2):
            sums.arrived(("P", h, n))
            total = total + rp[h, n].astype(F32)
        out[h * 128 : h * 128 + 128, :] = total.astype(BF16)

    links.finish()
    sums.finish()
    for copy in waits:
        copy.wait_send()
    pl.when(s < BLOCKS - 1)(halo.wait_send)
    for i, copy in enumerate(returns):
        pl.when(s != i)(copy.wait_send)


def per_device(tokens, in_weight, short_taps, filter_in, filter_out, rates, skip, out_weight):
    forward, inverse, feats = tables(4096)
    vmem = pl.BlockSpec(memory_space=pltpu.VMEM)
    hbm = pl.BlockSpec(memory_space=pl.ANY)
    dma = pltpu.SemaphoreType.DMA
    square = (BLOCK, BLOCK)
    scratch = [
        pltpu.VMEM((3, 3, BLOCK), F32),
        pltpu.VMEM((33, 64), F32),
        pltpu.VMEM((64, BLOCK), F32),
        pltpu.VMEM((1, BLOCK), F32),
        pltpu.VMEM((1, BLOCK), F32),
        pltpu.VMEM((16, *square), BF16),
        pltpu.VMEM((16, 3, *square), BF16),
        pltpu.VMEM((16, *square), BF16),
        pltpu.VMEM((FEAT_ROWS, 4096), F32),
        pltpu.VMEM((2, BLOCK, FREQS), BF16),
        pltpu.VMEM((2, FREQS, BLOCK), BF16),
        pltpu.VMEM((3, *square), F32),
        pltpu.VMEM((128, 128), F32),
        pltpu.VMEM((BLOCK, 64), F32),
        pltpu.VMEM((BLOCK, 128), F32),
        pltpu.VMEM((BLOCK, 128), F32),
        pltpu.VMEM(square, F32),
        pltpu.VMEM((GROUP + BLOCK, FREQS), F32),
        pltpu.VMEM((BLOCK + LAG_PAD, BLOCK), F32),
        pltpu.VMEM((BLOCK + LAG_PAD, BLOCK), F32),
        pltpu.VMEM((BLOCK + LAG_PAD, BLOCK), F32),
        pltpu.VMEM((3, EDGE, BLOCK), BF16),
        pltpu.VMEM((3, EDGE, BLOCK), BF16),
        pltpu.VMEM((3, 16 + BLOCK, BLOCK), F32),
        pltpu.VMEM(square, F32),
        pltpu.VMEM(square, F32),
        pltpu.VMEM((BLOCKS, GROUP, BLOCK), BF16),
        pltpu.VMEM((BLOCKS, GROUP, BLOCK), BF16),
        pltpu.VMEM((LAG_PAD + BLOCK, FREQS), F32),
        pltpu.VMEM((BLOCK, FREQS), F32),
        pltpu.VMEM((BLOCKS, GROUP, BLOCK), BF16),
        pltpu.VMEM((BLOCKS, GROUP, BLOCK), BF16),
        pltpu.VMEM(square, BF16),
        pltpu.VMEM((16, *square), F32),
        pltpu.VMEM((2, 4, 3, 128, BLOCK), BF16),
        pltpu.VMEM((2, 4, 2, 64, BLOCK), BF16),
        pltpu.VMEM((2, 4, 2, 128, BLOCK), BF16),
        pltpu.VMEM((2, 3, 128, BLOCK), BF16),
        pltpu.VMEM((2, 3, 128, BLOCK), BF16),
        pltpu.VMEM((2, 128, BLOCK), F32),
        pltpu.SemaphoreType.REGULAR((4,)),
        dma((9,)),
        dma((16,)),
        dma((16,)),
        dma((53,)),
        dma((53,)),
        dma((1,)),
        dma((1,)),
        dma((16,)),
        dma((16,)),
        dma((16,)),
        dma((16,)),
        dma((54,)),
        dma((54,)),
    ]
    return pl.pallas_call(
        kernel,
        out_shape=pltpu.VMEM(square, BF16),
        in_specs=[hbm] * 11,
        out_specs=vmem,
        scratch_shapes=scratch,
        compiler_params=pltpu.CompilerParams(
            collective_id=0, has_side_effects=True, vmem_limit_bytes=56 * 1024 * 1024
        ),
        name="hyena",
    )(
        tokens,
        jnp.transpose(in_weight, (1, 0, 2)),
        short_taps,
        filter_in,
        filter_out,
        rates.reshape(1, BLOCK),
        skip.reshape(1, BLOCK),
        out_weight,
        jnp.asarray(feats),
        jnp.asarray(forward),
        jnp.asarray(inverse),
    )


def solution(mesh):
    placed = (
        P("seq", "chan"),
        P(None, None, "chan"),
        P(None, None, "chan"),
        P(),
        P(None, "chan"),
        P("chan"),
        P("chan"),
        P("chan", None),
    )
    return jax.shard_map(
        per_device, mesh=mesh, in_specs=placed, out_specs=P("seq", "chan"), check_vma=False
    )
```

```python
import functools
import math

import jax
import jax.numpy as jnp
import ml_dtypes
import numpy as np
from jax import lax
from jax.experimental import pallas as pl
from jax.experimental.pallas import tpu as pltpu
from jax.sharding import PartitionSpec as P

BLOCK = 256
GROUP = 16
BLOCKS = 16
FREQS = 2 * BLOCK
FEAT_ROWS = 40
EDGE = 16
LAG_STEP = 4
LAG_PAD = (LAG_STEP - 1) * GROUP
ORDER = (8, 7, 9, 6, 10, 5, 11, 4, 12, 3, 13, 2, 14, 1, 15)
MESH_ID = pl.DeviceIdType.MESH
F32 = jnp.float32
BF16 = jnp.bfloat16


def split_two(values):
    high = values.astype(ml_dtypes.bfloat16)
    low = (values - high.astype(np.float64)).astype(ml_dtypes.bfloat16)
    return np.stack([high, low])


@functools.cache
def tables(total):
    row = np.arange(BLOCK)
    freq = np.arange(BLOCK)
    angle = 2.0 * np.pi * ((row[:, None] * freq[None, :]) % FREQS) / FREQS
    imag = -np.sin(angle)
    imag[:, 0] = 1.0 - 2.0 * (row % 2)
    forward = np.concatenate([np.cos(angle), imag], axis=1)
    angle = 2.0 * np.pi * ((freq[:, None] * (row[None, :] + BLOCK)) % FREQS) / FREQS
    real_rows = 2.0 * np.cos(angle)
    real_rows[0] = 1.0
    imag_rows = -2.0 * np.sin(angle)
    imag_rows[0] = 1.0 - 2.0 * (row % 2)
    inverse = np.concatenate([real_rows, imag_rows], axis=0) / FREQS
    place = np.arange(total)
    count = 16
    rates = 1 + np.arange(count) * (total // 4 - 1) // (count - 1)
    phase = (place[None, :] * rates[:, None]) % total
    turn = 2.0 * np.pi * phase / total
    feats = np.zeros((FEAT_ROWS, total), np.float32)
    feats[0] = place / total
    feats[1 : 1 + count] = np.cos(turn)
    feats[1 + count : 1 + 2 * count] = np.sin(turn)
    return split_two(forward), split_two(inverse), feats


def sine(x):
    turns = jnp.round(x * (1.0 / math.pi))
    r = x - turns * 3.140625
    r = r - turns * 0.0009670257568359375
    r = r - turns * 6.2771141529083252e-07
    odd = turns - 2.0 * jnp.floor(turns * 0.5)
    z = r * r
    poly = 1.0 / 6227020800.0
    for term in (-39916800.0, 362880.0, -5040.0, 120.0, -6.0):
        poly = poly * z + 1.0 / term
    value = r + r * z * poly
    return value * (1.0 - 2.0 * odd)


def dot(a, b):
    return jnp.dot(a, b, preferred_element_type=F32)


def halves(x):
    high = x.astype(BF16)
    return high, (x - high.astype(F32)).astype(BF16)


def slot(h, first, second):
    dx, dy = (first, second) if h == 0 else (second, first)
    return (dy % 4) * 4 + dx % 4


def rows(h, part):
    base = h * 128
    cut = EDGE if h else 0
    return {"f": (base, 128 - cut), "q1": (base, 64), "q2": (base + 64, 64 - cut)}[part]


class Links:
    def __init__(self, send, recv):
        self.send, self.recv, self.known = send, recv, {}

    def start(self, name, src, dst, device):
        index = len(self.known)
        copy = pltpu.make_async_remote_copy(
            src_ref=src,
            dst_ref=dst,
            send_sem=self.send.at[index],
            recv_sem=self.recv.at[index],
            device_id=device,
            device_id_type=MESH_ID,
        )
        copy.start()
        self.known[name] = copy

    def arrived(self, name):
        self.known[name].wait_recv()

    def finish(self):
        for copy in self.known.values():
            copy.wait_send()


def kernel(
    tok, win, taps_in, fin_in, fout_in, rates_in, skip_in, wout, feats, fmat, gmat,
    out,
    taps, fin, fout, rates, skip, xbuf, wbuf, wo, featbuf, fbuf, gbuf, acc, finp, fot, ratecol, skipcol, fs, aspec, sre, sim, sre2,
    edge_out, edge_in, pf, qbuf, drv, sbuf, dbuf, xs, ys, cbuf, rbuf, gated,
    part, snd, rq, rh, psnd, rp, red,
    word_sem, local_sem, w_sem, wo_sem, ag_send, ag_recv, halo_send, halo_recv, a_send, a_recv, b_send, b_recv, rs_send, rs_recv,
):
    s = lax.axis_index("seq")
    c = lax.axis_index("chan")
    x, y = lax.rem(c, 4), lax.div(c, 4)
    spots = [(dx, dy) for dy in range(4) for dx in range(4)]

    def chan_at(dx, dy):
        return lax.rem(y + dy + 4, 4) * 4 + lax.rem(x + dx + 4, 4)

    def neighbour(h, stage, sign):
        along_x = (h == 0) == (stage == 0)
        return {"chan": chan_at(sign, 0) if along_x else chan_at(0, sign)}

    z, core = lax.div(s, 2), lax.rem(s, 2)

    def plane(step):
        return {"seq": lax.rem(z + step + 8, 8) * 2 + core}

    sibling = {"seq": z * 2 + 1 - core}
    barrier = pltpu.get_barrier_semaphore()
    near = [{"chan": chan_at(step, 0)} for step in (1, -1, 2)]
    near += [{"chan": chan_at(0, step)} for step in (1, -1, 2)]
    near += [sibling]
    for device in near:
        pl.semaphore_signal(barrier, inc=1, device_id=device, device_id_type=MESH_ID)

    def planes(step):
        return (z < 8 - step).astype(jnp.int32) + (z >= step).astype(jnp.int32)

    def greet(semaphore, step):
        for there, sign in ((z < 8 - step, step), (z >= step, -step)):

            @pl.when(there)
            def _():
                pl.semaphore_signal(semaphore, inc=1, device_id=plane(sign), device_id_type=MESH_ID)

    greet(barrier, 1)

    small = [
        pltpu.make_async_copy(src, dst, local_sem.at[4 + n])
        for n, (src, dst) in enumerate(
            ((fin_in, fin), (fout_in, fout), (rates_in, rates), (skip_in, skip), (taps_in, taps))
        )
    ]
    for copy in small:
        copy.start()
    own = pltpu.make_async_copy(tok, xbuf.at[0], local_sem.at[0])
    own.start()
    order = [(0, 0), (1, 0), (3, 0), (0, 1), (0, 3), (2, 0), (0, 2), (1, 1), (1, 3), (3, 1), (3, 3),
             (1, 2), (2, 1), (3, 2), (2, 3), (2, 2)]
    w_copies = {}
    feat_copy = pltpu.make_async_copy(feats, featbuf, local_sem.at[1])
    f_copy = pltpu.make_async_copy(fmat, fbuf, local_sem.at[2])
    g_copy = pltpu.make_async_copy(gmat, gbuf, local_sem.at[3])
    feat_copy.start()

    def start_weights(first, last):
        for n in range(first, last):
            dx, dy = order[n]
            at = pl.ds(pl.multiple_of(chan_at(-dx, -dy) * BLOCK, BLOCK), BLOCK)
            w_copies[dx, dy] = pltpu.make_async_copy(win.at[:, at, :], wbuf.at[n], w_sem.at[n])
            w_copies[dx, dy].start()

    start_weights(0, 1)
    wo_copies = {}

    pl.semaphore_wait(barrier, len(near) + planes(1))

    def tell(n):
        if n == 3:
            pl.semaphore_signal(word_sem.at[n], inc=1, device_id=sibling, device_id_type=MESH_ID)
        else:
            greet(word_sem.at[n], 1 << n)

    def hear(n):
        pl.semaphore_wait(word_sem.at[n], 1 if n == 3 else planes(1 << n))

    links = Links(ag_send, ag_recv)

    def push(name, h, frm, to, piece, stage, sign):
        start, size = rows(h, piece)
        here = xbuf.at[slot(h, *frm), pl.ds(start, size), :]
        there = xbuf.at[slot(h, *to), pl.ds(start, size), :]
        links.start((name, h), here, there, neighbour(h, stage, sign))

    def take(*names):
        for name in names:
            for h in (0, 1):
                links.arrived((name, h))

    def multiply(blocks, first=False):
        for dx, dy in blocks:
            if (dx, dy) == (0, 0):
                w_copies[dx, dy].wait()
        for j in range(3):
            total = None if first else acc[j]
            for dx, dy in blocks:
                term = dot(xbuf[dy * 4 + dx], wbuf[order.index((dx, dy)), j])
                total = term if total is None else total + term
            acc[j] = total

    own.wait()
    tell(0)
    for h in (0, 1):
        push("P2", h, (0, 0), (2, 0), "f", 0, 2)
        push("P0+", h, (0, 0), (1, 0), "f", 0, 1)
        push("P0-", h, (0, 0), (3, 0), "f", 0, -1)
    for h in (0, 1):
        push("Q00+", h, (0, 0), (0, 1), "f", 1, 1)
        push("Q00-", h, (0, 0), (0, 3), "f", 1, -1)

    edge = pl.ds(BLOCK - EDGE, EDGE)
    for step in (1, 2, 3):
        links.start(
            ("EP", step),
            xbuf.at[0, edge, :],
            xbuf.at[step * (1 + 3 * core), edge, :],
            {"chan": chan_at(step * (1 - core), step * core)},
        )
    start_weights(1, 16)
    f_copy.start()

    for copy in small:
        copy.wait()
    finp[...] = jnp.zeros_like(finp)
    finp[0:33, 0:64] = fin[...]
    fin_t = jnp.transpose(finp[...])[0:64, 0:FEAT_ROWS]
    fot[...] = jnp.transpose(fout[...])
    ratecol[...] = jnp.transpose(jnp.broadcast_to(rates[...], (128, BLOCK)))
    skipcol[...] = jnp.transpose(jnp.broadcast_to(skip[...], (128, BLOCK)))
    mine = pl.ds(pl.multiple_of(s * GROUP, GROUP), GROUP)
    fo = fot[mine, :]
    rate = ratecol[mine, :]
    rate = jnp.concatenate([rate] * 4, axis=1)
    scale = jnp.sqrt(rate)
    feat_copy.wait()

    def filter_piece(n, carry):
        at = pl.ds(pl.multiple_of(n * 512, 512), 512)
        arg = jnp.dot(fin_t, featbuf[:, at], precision=lax.Precision.HIGHEST, preferred_element_type=F32)
        shaped = jnp.dot(fo, sine(arg), precision=lax.Precision.HIGHEST, preferred_element_type=F32)
        place = (lax.broadcasted_iota(jnp.int32, (GROUP, 512), 1) + n * 512).astype(F32)
        value = shaped * scale * jnp.exp(-rate * place)
        fs[pl.ds(pl.multiple_of(n * 32, 32), GROUP), :] = value[:, :BLOCK]
        fs[pl.ds(pl.multiple_of(n * 32 + 16, 16), GROUP), :] = value[:, BLOCK:]
        return carry

    lax.fori_loop(0, 4, filter_piece, 0)
    multiply([(0, 0)], first=True)

    take("P0+", "P0-")
    for h in (0, 1):
        for dp in (1, 3):
            push(f"Q{dp}0+", h, (dp, 0), (dp, 1), "f", 1, 1)
            push(f"Q{dp}0-", h, (dp, 0), (dp, 3), "f", 1, -1)
    take("P2")
    for h in (0, 1):
        push("Q20+", h, (2, 0), (2, 1), "f", 1, 1)
        push("Q20-", h, (2, 0), (2, 3), "f", 1, -1)
    take("Q00+", "Q00-")
    for h in (0, 1):
        push("Q01+", h, (0, 1), (0, 2), "q1", 1, 1)
        push("Q01-", h, (0, 3), (0, 2), "q2", 1, -1)
    for step in (1, 2, 3):
        links.arrived(("EP", step))
    for step in (1, 2, 3):
        for k in range(4):
            links.start(
                ("EQ", step, k),
                xbuf.at[k * (1 + 3 * core), edge, :],
                xbuf.at[k * (1 + 3 * core) + step * (4 - 3 * core), edge, :],
                {"chan": chan_at(step * core, step * (1 - core))},
            )
    hear(0)
    tell(1)
    lax.fori_loop(4, 8, filter_piece, 0)
    for dp in (1, 3):
        take(f"Q{dp}0+", f"Q{dp}0-")
        for h in (0, 1):
            push(f"Q{dp}1+", h, (dp, 1), (dp, 2), "q1", 1, 1)
            push(f"Q{dp}1-", h, (dp, 3), (dp, 2), "q2", 1, -1)

    take("Q20+", "Q20-")
    for h in (0, 1):
        push("Q21+", h, (2, 1), (2, 2), "q1", 1, 1)
        push("Q21-", h, (2, 3), (2, 2), "q2", 1, -1)

    hear(1)
    tell(2)

    for step in (1, 2, 3):
        for k in range(4):
            links.arrived(("EQ", step, k))
    for dx, dy in order[1:]:
        w_copies[dx, dy].wait()
    for j in range(3):
        total = None
        for dx, dy in order:
            term = dot(xbuf[dy * 4 + dx, BLOCK - EDGE :, :], wbuf[order.index((dx, dy)), j])
            total = term if total is None else total + term
        edge_out[j] = total.astype(BF16)
    halo = pltpu.make_async_remote_copy(
        src_ref=edge_out,
        dst_ref=edge_in,
        send_sem=halo_send.at[0],
        recv_sem=halo_recv.at[0],
        device_id={"seq": lax.rem(s + 1, BLOCKS)},
        device_id_type=MESH_ID,
    )
    pl.when(s < BLOCKS - 1)(halo.start)
    g_copy.start()
    for n, (dx, dy) in enumerate(spots):
        at = pl.ds(pl.multiple_of(chan_at(dx, dy) * BLOCK, BLOCK), BLOCK)
        wo_copies[dx, dy] = pltpu.make_async_copy(wout.at[:, at], wo.at[n], wo_sem.at[n])
        wo_copies[dx, dy].start()

    take("Q01+", "Q01-")
    multiply(order[1:11])
    hear(2)
    tell(3)
    for h, dp, block in ((0, 1, (1, 2)), (1, 1, (2, 1)), (0, 3, (3, 2)), (1, 3, (2, 3))):
        links.arrived((f"Q{dp}1+", h))
        links.arrived((f"Q{dp}1-", h))
        multiply([block])
    take("Q21+", "Q21-")
    multiply([(2, 2)])

    for j in range(3):
        pf[j, 16:, :] = acc[j].astype(BF16).astype(F32)

    def short(start, size):
        branch = []
        for j in range(3):
            value = taps[0, pl.ds(j, 1), :] * pf[j, pl.ds(16 + start, size), :]
            value = value + taps[1, pl.ds(j, 1), :] * pf[j, pl.ds(15 + start, size), :]
            branch.append(value + taps[2, pl.ds(j, 1), :] * pf[j, pl.ds(14 + start, size), :])
        qbuf[pl.ds(start, size), :] = branch[0]
        drv[pl.ds(start, size), :] = branch[1] * branch[2]

    pl.when(s > 0)(halo.wait_recv)

    @pl.when(s == 0)
    def _():
        edge_in[...] = jnp.zeros_like(edge_in)

    for j in range(3):
        pf[j, 0:16, :] = edge_in[j].astype(F32)
    for start in range(0, BLOCK, 32):
        short(start, 32)

    sbuf[...] = jnp.transpose(drv[...]).astype(BF16).reshape(BLOCKS, GROUP, BLOCK)

    def message(src, dst, send, recv, other):
        return pltpu.make_async_remote_copy(
            src_ref=src,
            dst_ref=dst.at[s],
            send_sem=send,
            recv_sem=recv.at[s],
            device_id={"seq": other},
            device_id_type=MESH_ID,
        )

    def got(j, buffer, send, recv):
        @pl.when(s != j)
        def _():
            pltpu.make_async_remote_copy(
                src_ref=buffer.at[j],
                dst_ref=buffer.at[j],
                send_sem=send.at[0],
                recv_sem=recv.at[j],
                device_id={"seq": lax.rem(s + 1, BLOCKS)},
                device_id_type=MESH_ID,
            ).wait_recv()

    hear(3)
    waits = []
    for k in ORDER:
        other = lax.rem(s + k, BLOCKS)
        copy = message(sbuf.at[other], dbuf, a_send.at[k], a_recv, other)
        copy.start()
        waits.append(copy)
    dbuf[pl.ds(s, 1)] = sbuf[pl.ds(s, 1)]
    f_copy.wait()
    aspec[0:GROUP, :] = jnp.zeros((GROUP, FREQS), F32)
    lane = lax.broadcasted_iota(jnp.int32, (GROUP, BLOCK), 1)
    parity = 1.0 - 2.0 * lax.rem(lane, 2).astype(F32)

    for table in (sre, sim, sre2):
        table[BLOCK:, :] = jnp.zeros((LAG_PAD, BLOCK), F32)

    def lag_piece(n, carry):
        before = pl.ds(pl.multiple_of(n * GROUP, GROUP), GROUP)
        after = pl.ds(pl.multiple_of(n * GROUP + GROUP, GROUP), GROUP)
        re = aspec[before, 0:BLOCK] + parity * aspec[after, 0:BLOCK]
        im = aspec[before, BLOCK:] + parity * aspec[after, BLOCK:]
        sre[before, :] = re
        sim[before, :] = jnp.where(lane == 0, 0.0, im)
        sre2[before, :] = jnp.where(lane == 0, im, re)
        return carry

    def lag_spectra(first, last):
        high, low = halves(fs[first * GROUP : last * GROUP, :])
        spectra = dot(high, fbuf[0]) + dot(low, fbuf[0]) + dot(high, fbuf[1])
        aspec[(first + 1) * GROUP : (last + 1) * GROUP, :] = spectra
        lax.fori_loop(first, last, lag_piece, 0)

    lag_spectra(0, 4)

    xs[0:LAG_PAD, :] = jnp.zeros((LAG_PAD, FREQS), F32)
    direct = skipcol[mine, :]
    direct = jnp.concatenate([direct, direct], axis=1)
    g_copy.wait()

    def spectrum(i):
        def lags(turn, total):
            re, im = total
            for d in range(LAG_STEP):
                d = turn * LAG_STEP + d
                at = pl.ds(pl.multiple_of((i - d) * GROUP + LAG_PAD, GROUP), GROUP)
                by = pl.ds(pl.multiple_of(d * GROUP, GROUP), GROUP)
                xr, xi = xs[at, 0:BLOCK], xs[at, BLOCK:]
                part_im = sim[by, :]
                re = re + (xr * sre[by, :] - xi * part_im)
                im = im + (xr * part_im + xi * sre2[by, :])
            return re, im

        zero = jnp.zeros((GROUP, BLOCK), F32)
        re, im = lax.fori_loop(0, (i + LAG_STEP) // LAG_STEP, lags, (zero, zero))
        ys[i * GROUP : (i + 1) * GROUP, 0:BLOCK] = re
        ys[i * GROUP : (i + 1) * GROUP, BLOCK:] = im

    returns = []
    for low_block, high_block in ((0, 4), (4, 8), (8, 16)):
        count = (high_block - low_block) * GROUP
        for j in range(low_block, high_block):
            got(j, dbuf, a_send, a_recv)
        some = slice(low_block * GROUP, high_block * GROUP)
        drive = dbuf[low_block:high_block].reshape(count, BLOCK)
        xs[LAG_PAD + some.start : LAG_PAD + some.stop, :] = dot(drive, fbuf[0]) + dot(drive, fbuf[1])
        for i in range(low_block, high_block):
            spectrum(i)
        high, low = halves(ys[some, :])
        both = dot(jnp.concatenate([high, low], axis=0), gbuf[0])
        conv = both[:count] + both[count:] + dot(high, gbuf[1])
        for i in range(low_block, high_block):
            value = conv[(i - low_block) * GROUP : (i - low_block + 1) * GROUP, :]
            cbuf[i] = (value + direct * dbuf[i].astype(F32)).astype(BF16)
            copy = message(cbuf.at[i], rbuf, b_send.at[i], b_recv, i)
            returns.append(copy)
            pl.when(s != i)(copy.start)
        if low_block == 0:
            lag_spectra(4, BLOCKS)
    rbuf[pl.ds(s, 1)] = cbuf[pl.ds(s, 1)]
    for j in range(BLOCKS):
        got(j, rbuf, b_send, b_recv)

    back = jnp.transpose(rbuf[...].reshape(BLOCK, BLOCK).astype(F32))
    gated[...] = (qbuf[...] * back).astype(BF16)

    sums = Links(rs_send, rs_recv)

    def project(dx, dy):
        wo_copies[dx, dy].wait()
        part[dy * 4 + dx] = dot(gated[...], wo[dy * 4 + dx])

    def half(h, dp, dq):
        return part.at[slot(h, dp, dq), pl.ds(h * 128, 128), :]

    column = (2, 1, 3, 0)

    def relay(h, e):
        snd[h, e, 0] = half(h, column[e], 2)[...].astype(BF16)
        sums.start(("Q1+", h, e), snd.at[h, e, 0, pl.ds(0, 64), :], rq.at[h, e, 0], neighbour(h, 1, 1))
        sums.start(("Q1-", h, e), snd.at[h, e, 0, pl.ds(64, 64), :], rq.at[h, e, 1], neighbour(h, 1, -1))

    for e in range(4):
        for h in (0, 1):
            if e or not h:
                project(*((column[e], 2) if h == 0 else (2, column[e])))
            relay(h, e)
    def pass_on(name, h, e, n, start, value):
        there = pl.ds(start, 64)
        snd[h, e, n, there, :] = value.astype(BF16)
        sums.start(
            (name, h, e, n), snd.at[h, e, n, there, :], rh.at[h, e, n - 1, there, :], neighbour(h, 1, 3 - 2 * n)
        )

    def free(e):
        for h in (0, 1):
            pass_on("free", h, e, 1, 64, half(h, column[e], 1)[64:128, :])
            pass_on("free", h, e, 2, 0, half(h, column[e], 3)[0:64, :])

    def joined(e):
        for h in (0, 1):
            sums.arrived(("Q1+", h, e))
            pass_on("joined", h, e, 1, 0, half(h, column[e], 1)[0:64, :] + rq[h, e, 0].astype(F32))
            sums.arrived(("Q1-", h, e))
            pass_on("joined", h, e, 2, 64, half(h, column[e], 3)[64:128, :] + rq[h, e, 1].astype(F32))

    free(0)
    for dx, dy in ((1, 1), (1, 3), (3, 1)):
        project(dx, dy)
    free(1)
    project(3, 3)
    free(2)
    for dx, dy in ((0, 1), (1, 0), (0, 3), (3, 0), (0, 0)):
        project(dx, dy)
    for e in (0, 1, 2):
        joined(e)
    free(3)
    joined(3)

    def reduced(h, e):
        for name in ("free", "joined"):
            for n in (1, 2):
                sums.arrived((name, h, e, n))
        return half(h, column[e], 0)[...] + rh[h, e, 0].astype(F32) + rh[h, e, 1].astype(F32)

    for e, sign in ((0, 2), (1, 1), (2, -1)):
        for h in (0, 1):
            psnd[h, e] = reduced(h, e).astype(BF16)
            sums.start(("P", h, e), psnd.at[h, e], rp.at[h, e], neighbour(h, 0, sign))
    for h in (0, 1):
        red[h] = reduced(h, 3)
    links.finish()
    sums.finish()
    for copy in waits:
        copy.wait_send()
    pl.when(s < BLOCKS - 1)(halo.wait_send)
    for i, copy in enumerate(returns):
        pl.when(s != i)(copy.wait_send)
    for h in (0, 1):
        total = red[h]
        for n in (0, 1, 2):
            sums.arrived(("P", h, n))
            total = total + rp[h, n].astype(F32)
        out[h * 128 : h * 128 + 128, :] = total.astype(BF16)


def per_device(tokens, in_weight, short_taps, filter_in, filter_out, rates, skip, out_weight):
    forward, inverse, feats = tables(4096)
    vmem = pl.BlockSpec(memory_space=pltpu.VMEM)
    hbm = pl.BlockSpec(memory_space=pl.ANY)
    dma = pltpu.SemaphoreType.DMA
    square = (BLOCK, BLOCK)
    scratch = [
        pltpu.VMEM((3, 3, BLOCK), F32),
        pltpu.VMEM((33, 64), F32),
        pltpu.VMEM((64, BLOCK), F32),
        pltpu.VMEM((1, BLOCK), F32),
        pltpu.VMEM((1, BLOCK), F32),
        pltpu.VMEM((16, *square), BF16),
        pltpu.VMEM((16, 3, *square), BF16),
        pltpu.VMEM((16, *square), BF16),
        pltpu.VMEM((FEAT_ROWS, 4096), F32),
        pltpu.VMEM((2, BLOCK, FREQS), BF16),
        pltpu.VMEM((2, FREQS, BLOCK), BF16),
        pltpu.VMEM((3, *square), F32),
        pltpu.VMEM((128, 128), F32),
        pltpu.VMEM((BLOCK, 64), F32),
        pltpu.VMEM((BLOCK, 128), F32),
        pltpu.VMEM((BLOCK, 128), F32),
        pltpu.VMEM(square, F32),
        pltpu.VMEM((GROUP + BLOCK, FREQS), F32),
        pltpu.VMEM((BLOCK + LAG_PAD, BLOCK), F32),
        pltpu.VMEM((BLOCK + LAG_PAD, BLOCK), F32),
        pltpu.VMEM((BLOCK + LAG_PAD, BLOCK), F32),
        pltpu.VMEM((3, EDGE, BLOCK), BF16),
        pltpu.VMEM((3, EDGE, BLOCK), BF16),
        pltpu.VMEM((3, 16 + BLOCK, BLOCK), F32),
        pltpu.VMEM(square, F32),
        pltpu.VMEM(square, F32),
        pltpu.VMEM((BLOCKS, GROUP, BLOCK), BF16),
        pltpu.VMEM((BLOCKS, GROUP, BLOCK), BF16),
        pltpu.VMEM((LAG_PAD + BLOCK, FREQS), F32),
        pltpu.VMEM((BLOCK, FREQS), F32),
        pltpu.VMEM((BLOCKS, GROUP, BLOCK), BF16),
        pltpu.VMEM((BLOCKS, GROUP, BLOCK), BF16),
        pltpu.VMEM(square, BF16),
        pltpu.VMEM((16, *square), F32),
        pltpu.VMEM((2, 4, 3, 128, BLOCK), BF16),
        pltpu.VMEM((2, 4, 2, 64, BLOCK), BF16),
        pltpu.VMEM((2, 4, 2, 128, BLOCK), BF16),
        pltpu.VMEM((2, 3, 128, BLOCK), BF16),
        pltpu.VMEM((2, 3, 128, BLOCK), BF16),
        pltpu.VMEM((2, 128, BLOCK), F32),
        pltpu.SemaphoreType.REGULAR((4,)),
        dma((9,)),
        dma((16,)),
        dma((16,)),
        dma((53,)),
        dma((53,)),
        dma((1,)),
        dma((1,)),
        dma((16,)),
        dma((16,)),
        dma((16,)),
        dma((16,)),
        dma((54,)),
        dma((54,)),
    ]
    return pl.pallas_call(
        kernel,
        out_shape=pltpu.VMEM(square, BF16),
        in_specs=[hbm] * 11,
        out_specs=vmem,
        scratch_shapes=scratch,
        compiler_params=pltpu.CompilerParams(
            collective_id=0, has_side_effects=True, vmem_limit_bytes=56 * 1024 * 1024
        ),
        name="hyena",
    )(
        tokens,
        jnp.transpose(in_weight, (1, 0, 2)),
        short_taps,
        filter_in,
        filter_out,
        rates.reshape(1, BLOCK),
        skip.reshape(1, BLOCK),
        out_weight,
        jnp.asarray(feats),
        jnp.asarray(forward),
        jnp.asarray(inverse),
    )


def solution(mesh):
    placed = (
        P("seq", "chan"),
        P(None, None, "chan"),
        P(None, None, "chan"),
        P(),
        P(None, "chan"),
        P("chan"),
        P("chan"),
        P("chan", None),
    )
    return jax.shard_map(
        per_device, mesh=mesh, in_specs=placed, out_specs=P("seq", "chan"), check_vma=False
    )
```
